512 devices in a mesh: shard: 32 (over y, x), replica: 16 (over z, core).
Axes of the slice: x: 4, y: 8, z: 8, core: 2. Of those that a mesh axis runs over, the one named last changes fastest.
Arguments:
- tokens: bfloat16 [65536, 6144], P(('shard', 'replica')), may hold values from -6 to 6
- weight: bfloat16 [512, 6144], P('shard'), may hold values from -0.078125 to 0.078125
- momentum: float32 [16, 512, 6144], P('replica', 'shard'), may hold values from -6 to 6
- gradient: bfloat16 [16, 512, 6144], P('replica', 'shard'), may hold values from -6 to 6
- indices: int32 [16, 512, 96, 4], P('replica', 'shard'), may hold values from 0 to 63, all different within a row
Outputs:
- projected: bfloat16 [65536, 512], P(('shard', 'replica'))
- new_momentum: float32 [16, 512, 6144], P('replica', 'shard')
The draws below stay inside these ranges and needn't reach their ends.
Inputs may be any that keep to these rules, and one draw needn't show every extreme that they name: The 4 indices of one replica, row and transform differ.
All inputs are finite; a program needn't handle non-finite values.
Results may differ from the reference program's by a relative error of at most 0.0054.
Values may be sent and summed in bfloat16 or wider, within the bound.
No kernel may reach another device: no remote copies, remote signals or barrier semaphores. Data moves between devices by JAX's collectives and lax.ppermute only.
A program may use at most 64 MiB of HBM per device.

```python
import math
import jax
import jax.numpy as jnp
from jax import lax

D = 6144
GROUP = 64
TOPK = 4
GROUPS = 96
ROWS = 512
REPLICAS = 16
TOKENS = 65536


def level_of(rng, extent, cuts, smallest, largest):
    factor_of = 1.0
    for dim, blocks in cuts:
        heights = jax.random.uniform(jax.random.fold_in(jax.random.fold_in(rng, 6), dim), (blocks,), jnp.float32, smallest / len(cuts), largest / len(cuts))
        factor_of = factor_of * jnp.repeat(jnp.exp(heights), extent[dim] // blocks).reshape((-1,) + (1,) * (len(extent) - 1 - dim))
    return factor_of


def choose_distinct(own_key, rows, number_of, top, lift):
    sequence = jax.random.permutation(jax.random.fold_in(own_key, 1), number_of)
    favour = sequence
    for power in range(3):
        favour = favour * favour // number_of
    favour = favour * lift // number_of
    lots = jax.random.randint(jax.random.fold_in(own_key, 2), (rows, number_of), 0, 4096) + favour
    fixed_rows = jax.random.permutation(jax.random.fold_in(own_key, 3), rows)[jnp.arange(number_of) % rows]
    lots = jnp.where(jnp.arange(rows)[:, None] == fixed_rows[None, :], 1 << 14, lots)
    score = lots * number_of + jnp.arange(number_of)
    return lax.top_k(score.astype(jnp.int32), top)[1].astype(jnp.int32)


def centred(stream_key, extent, deviation, reach, split=(), kind=jnp.bfloat16):
    array = jax.random.normal(stream_key, extent, jnp.float32) * deviation
    if len(split) > 0:
        array = level_of(stream_key, extent, split, -0.22, 0.18) * array
    return jnp.clip(array, min=-reach, max=reach).astype(kind)


def setup_inputs(seed: int = 0) -> dict:
    splits = jax.random.split(jax.random.key(seed), 6)
    return {
        "tokens": centred(splits[0], (TOKENS, D), 1.0, 6.0, ((0, 512),)),
        "weight": centred(splits[1], (ROWS, D), D ** -0.5, 0.078125, ((0, 32),)),
        "momentum": centred(splits[2], (REPLICAS, ROWS, D), 1.0, 6.0, ((0, 16), (1, 32)), jnp.float32),
        "gradient": centred(splits[3], (REPLICAS, ROWS, D), 1.0, 6.0, ((0, 16), (1, 32))),
        "indices": choose_distinct(splits[4], REPLICAS * ROWS * GROUPS, GROUP, TOPK, 0).reshape((REPLICAS, ROWS, GROUPS, TOPK)),
    }


decay_rate = 0.999
step_size = 0.01

def cosine_table():
    freq = jnp.arange(GROUP, dtype=jnp.float32)[:, None]
    place = jnp.arange(GROUP, dtype=jnp.float32)[None, :]
    values = jnp.cos(math.pi * (2.0 * place + 1.0) * freq / (2.0 * GROUP)) * math.sqrt(2.0 / GROUP)
    return values * jnp.where(freq == 0, math.sqrt(0.5), 1.0)

def forward_spectra(field, cosine):
    height = field.shape[0]
    flat = jnp.dot(field.reshape(-1, GROUP), cosine.T, precision=lax.Precision.HIGHEST)
    return flat.reshape(height, -1, GROUP)

def inverse_field(spectra, cosine):
    height = spectra.shape[0]
    flat = jnp.dot(spectra.reshape(-1, GROUP), cosine, precision=lax.Precision.HIGHEST)
    return flat.reshape(height, -1)

def select_hot(chosen):
    return (chosen[..., None] == jnp.arange(GROUP, dtype=jnp.int32)).astype(jnp.float32)

def decode(shipped, chosen):
    return lax.optimization_barrier(jnp.sum(shipped.astype(jnp.float32)[..., None] * select_hot(chosen), axis=2))

def local_step(momentum, gradient, chosen, cosine):
    blended = decay_rate * momentum + gradient.astype(jnp.float32)
    spectra = forward_spectra(blended, cosine)
    onehot = select_hot(chosen)
    picked = lax.optimization_barrier(jnp.sum(spectra[:, :, None, :] * onehot, axis=3))
    kept_part = lax.optimization_barrier(jnp.sum(picked[..., None] * onehot, axis=2))
    remain = blended - inverse_field(kept_part, cosine)
    return (remain, picked.astype(jnp.bfloat16))

def reference(tokens, weight, momentum, gradient, indices):
    cosine = cosine_table()
    new_momentum, shipped = lax.map(lambda members: local_step(members[0], members[1], members[2], cosine), (momentum, gradient, indices))

    def accumulate(running, members):
        return (running + decode(members[0], members[1]), None)
    zeros_start = jnp.zeros((weight.shape[0], GROUPS, GROUP), jnp.float32)
    spectra_sum, unused = lax.scan(accumulate, zeros_start, (shipped, indices))
    update = inverse_field(spectra_sum, cosine)
    renewed = (weight.astype(jnp.float32) - step_size * update).astype(jnp.bfloat16)
    projected = jnp.dot(tokens, renewed.T, preferred_element_type=jnp.float32).astype(jnp.bfloat16)
    return (projected, new_momentum)
```

```python
import numpy as np

import jax
import jax.numpy as jnp
from jax import lax
from jax.experimental import pallas as pl
from jax.experimental.pallas import tpu as pltpu
from jax.sharding import PartitionSpec as P

GROUP = 64
TOPK = 4
DECAY = 0.999
STEP = 0.01
PAIR = 2 * GROUP
XS = 4
YS = 8
F32 = jnp.float32
BF16 = jnp.bfloat16
HIGH = lax.Precision.HIGHEST


def pair_table():
    k = np.arange(GROUP, dtype=np.float64)[:, None]
    n = np.arange(GROUP, dtype=np.float64)[None, :]
    c = np.cos(np.pi * (2.0 * n + 1.0) * k / (2.0 * GROUP)) * np.sqrt(2.0 / GROUP)
    c = c * np.where(k == 0, np.sqrt(0.5), 1.0)
    both = np.zeros((PAIR, PAIR), np.float64)
    both[:GROUP, :GROUP] = c
    both[GROUP:, GROUP:] = c
    return both.astype(np.float32)


def contract(a, b, da, db):
    return lax.dot_general(a, b, (((da,), (db,)), ((), ())), precision=HIGH, preferred_element_type=F32)


def step_kernel(momentum, gradient, index, table, new_momentum, send):
    rows, width = momentum.shape[1:]
    pairs = width // PAIR
    lanes = pairs * rows
    blended = DECAY * momentum[0] + gradient[0].astype(F32)
    stacked = jnp.concatenate([blended[:, p * PAIR : (p + 1) * PAIR] for p in range(pairs)], axis=0)
    spectra = contract(table[...], stacked, 1, 1)
    freq = lax.broadcasted_iota(jnp.int32, (GROUP, lanes), 0)
    values, kept = [], []
    for side in range(2):
        part = spectra[side * GROUP : (side + 1) * GROUP]
        keep = jnp.zeros_like(part)
        for j in range(TOPK):
            hot = freq == index[side * TOPK + j][None, :]
            one = jnp.where(hot, part, 0.0)
            values.append(jnp.sum(one, axis=0, keepdims=True))
            keep = keep + one
        kept.append(keep)
    field = contract(jnp.concatenate(kept, axis=0), table[...], 0, 0)
    for p in range(pairs):
        at = slice(p * PAIR, (p + 1) * PAIR)
        new_momentum[0, :, at] = blended[:, at] - field[p * rows : (p + 1) * rows]
    message = jnp.concatenate(values + [index[...].astype(F32)], axis=0).astype(BF16)
    for r in range(send.shape[0]):
        half = r % 2
        send[r] = message[:, half * lanes // 2 : (half + 1) * lanes // 2]


def renew_kernel(received, weight, table, renewed):
    replicas, _, lanes = received.shape
    rows = weight.shape[0]
    half = weight.shape[1] // 2
    core = lax.axis_index("replica") % 2
    freq = lax.broadcasted_iota(jnp.int32, (GROUP, 128), 0).astype(F32)
    columns = []
    for c in range(lanes // 128):
        at = slice(c * 128, (c + 1) * 128)
        sums = [jnp.zeros((GROUP, 128), F32) for _ in range(2)]
        for r in range(replicas):
            message = received[r, :, at].astype(F32)
            for side in range(2):
                for j in range(TOPK):
                    row = side * TOPK + j
                    sums[side] = sums[side] + jnp.where(
                        freq == message[8 + row][None, :], message[row][None, :], 0.0
                    )
        columns.append(jnp.concatenate(sums, axis=0))
    field = contract(jnp.concatenate(columns, axis=1), table[...], 0, 0)
    old = weight[:, pl.ds(pl.multiple_of(core * half, 128), half)].astype(F32)
    per = half // XS // PAIR
    for x in range(XS):
        for p in range(per):
            q = x * per + p
            new = old[:, q * PAIR : (q + 1) * PAIR] - STEP * field[q * rows : (q + 1) * rows]
            new = new.astype(BF16)
            for y in range(YS):
                renewed[y * XS + x, :, p * PAIR : (p + 1) * PAIR] = new


def product_kernel(t0, t1, t2, t3, window, mine, other):
    count = mine.shape[1]
    for d, tokens in enumerate((t0, t1, t2, t3)):
        out = lax.dot_general(
            tokens[...], window[...], (((1,), (1,)), ((), ())), preferred_element_type=F32
        )
        mine[d] = out[:count]
        other[d] = out[count:].astype(BF16)


def order_kernel(mine, arrived, out):
    x = lax.axis_index("shard") % XS
    for d in range(XS):
        out[(x + XS - d) % XS] = (mine[d] + arrived[d].astype(F32)).astype(BF16)


def finish_kernel(parts, out):
    total = parts[0].astype(F32)
    for x in range(1, XS):
        total = total + parts[x].astype(F32)
    out[...] = total.astype(BF16)


def call(kernel, out, *args, flops=0):
    out_list = jax.tree.leaves(out)
    moved = sum(a.size * a.dtype.itemsize for a in args) + sum(o.size * o.dtype.itemsize for o in out_list)
    return pl.pallas_call(
        kernel,
        out_shape=out,
        in_specs=[pl.BlockSpec(memory_space=pltpu.VMEM)] * len(args),
        out_specs=jax.tree.map(lambda _: pl.BlockSpec(memory_space=pltpu.VMEM), out),
        compiler_params=pltpu.CompilerParams(vmem_limit_bytes=40 * 1024 * 1024),
        cost_estimate=pl.CostEstimate(flops=flops, bytes_accessed=moved, transcendentals=0),
    )(*args)


def local(tokens, weight, momentum, gradient, indices):
    count, width = tokens.shape
    rows = weight.shape[0]
    half, piece = width // 2, width // 2 // XS
    table = jnp.asarray(pair_table())
    core = lax.axis_index("replica") % 2
    x = lax.axis_index("shard") % XS
    replicas = lax.axis_size("replica")
    shards = lax.axis_size("shard")

    with jax.named_scope("tokens_core"):
        away = lax.dynamic_slice(tokens, (0, (1 - core) * half), (count, half))
        here = lax.dynamic_slice(tokens, (0, core * half), (count, half))
        came = lax.ppermute(away, "replica", [(i, i ^ 1) for i in range(replicas)])

    with jax.named_scope("local_step"):
        lanes = width // PAIR * rows
        index = indices[0].reshape(rows, width // PAIR, 2, TOPK).transpose(2, 3, 1, 0).reshape(2 * TOPK, lanes)
        new_momentum, send = call(
            step_kernel,
            (
                jax.ShapeDtypeStruct(momentum.shape, F32),
                jax.ShapeDtypeStruct((replicas, 4 * TOPK, lanes // 2), BF16),
            ),
            momentum,
            gradient,
            index,
            table,
            flops=10**8,
        )

    with jax.named_scope("tokens_x"):
        blocks = []
        for d in range(XS):
            start = (x + d) % XS * piece
            block = jnp.concatenate(
                [lax.dynamic_slice(a, (0, start), (count, piece)) for a in (here, came)], axis=0
            )
            if d > 0:
                block = lax.ppermute(
                    block, "shard", [(s, s // XS * XS + (s + d) % XS) for s in range(shards)]
                )
            blocks.append(block)

    with jax.named_scope("exchange"):
        received = lax.all_to_all(send, "replica", 0, 0)
    with jax.named_scope("renew"):
        renewed = call(
            renew_kernel, jax.ShapeDtypeStruct((shards, rows, piece), BF16), received, weight, table, flops=10**8
        )
    with jax.named_scope("window"):
        window = lax.all_to_all(renewed, "shard", 0, 0).reshape(shards * rows, piece)
    with jax.named_scope("product"):
        shape = (XS, count, shards * rows)
        mine, other = call(
            product_kernel,
            (jax.ShapeDtypeStruct(shape, F32), jax.ShapeDtypeStruct(shape, BF16)),
            *blocks,
            window,
            flops=2 * 1024 * 768 * 512,
        )
    with jax.named_scope("sum_core"):
        arrived = lax.ppermute(other, "replica", [(i, i ^ 1) for i in range(replicas)])
        ordered = call(order_kernel, jax.ShapeDtypeStruct(shape, BF16), mine, arrived)
    with jax.named_scope("sum_x"):
        groups = [[y * XS + i for i in range(XS)] for y in range(YS)]
        parts = lax.all_to_all(ordered, "shard", 0, 0, axis_index_groups=groups)
        projected = call(finish_kernel, jax.ShapeDtypeStruct(shape[1:], BF16), parts)
    return projected, new_momentum


def solution(mesh):
    in_specs = (
        P(("shard", "replica"), None),
        P("shard", None),
        P("replica", "shard", None),
        P("replica", "shard", None),
        P("replica", "shard", None, None),
    )
    out_specs = (P(("shard", "replica"), None), P("replica", "shard", None))
    return jax.shard_map(local, mesh=mesh, in_specs=in_specs, out_specs=out_specs, check_vma=False)
```

```python
import numpy as np

import jax
import jax.numpy as jnp
from jax import lax
from jax.experimental import pallas as pl
from jax.experimental.pallas import tpu as pltpu
from jax.sharding import PartitionSpec as P

GROUP = 64
TOPK = 4
DECAY = 0.999
STEP = 0.01
PAIR = 2 * GROUP
XS = 4
YS = 8
MEMBERS = 2 * XS
VMEM_BYTES = 60 * 1024 * 1024
F32 = jnp.float32
BF16 = jnp.bfloat16
HIGH = lax.Precision.HIGHEST


def pair_table():
    k = np.arange(GROUP, dtype=np.float64)[:, None]
    n = np.arange(GROUP, dtype=np.float64)[None, :]
    c = np.cos(np.pi * (2.0 * n + 1.0) * k / (2.0 * GROUP)) * np.sqrt(2.0 / GROUP)
    c = c * np.where(k == 0, np.sqrt(0.5), 1.0)
    both = np.zeros((PAIR, PAIR), np.float64)
    both[:GROUP, :GROUP] = c
    both[GROUP:, GROUP:] = c
    return both.astype(np.float32)


def contract(a, b, da, db):
    return lax.dot_general(a, b, (((da,), (db,)), ((), ())), precision=HIGH, preferred_element_type=F32)


def swap_kernel(t0, t1, t2, t3, away):
    core = lax.axis_index("replica") % 2
    for d, tokens in enumerate((t0, t1, t2, t3)):
        away[d] = tokens[1 - core]


def lay_out(indices, lanes):
    rows, _, groups = indices.shape
    spread = lax.broadcasted_iota(jnp.int32, (rows, lanes), 1) % rows
    spread = jnp.where(spread == lax.broadcasted_iota(jnp.int32, (rows, lanes), 0), 1.0, 0.0).astype(BF16)
    pair = lax.broadcasted_iota(jnp.int32, (groups, lanes), 1) // rows
    transform = lax.broadcasted_iota(jnp.int32, (groups, lanes), 0)
    spreads = [
        lax.dot_general(
            indices[:, j, :].astype(F32).astype(BF16), spread, (((0,), (0,)), ((), ())), preferred_element_type=F32
        )
        for j in range(TOPK)
    ]
    return [
        jnp.sum(jnp.where(transform == 2 * pair + side, spreads[j], 0.0), axis=0, keepdims=True)
        for side in range(2)
        for j in range(TOPK)
    ]


def choose(momentum, gradient, indices, table):
    rows, width = momentum.shape
    pairs = width // PAIR
    lanes = pairs * rows
    blended = DECAY * momentum + gradient.astype(F32)
    stacked = jnp.concatenate([blended[:, p * PAIR : (p + 1) * PAIR] for p in range(pairs)], axis=0)
    spectra = contract(table, stacked, 1, 1)
    freq = lax.broadcasted_iota(jnp.int32, (GROUP, lanes), 0).astype(F32)
    index = lay_out(indices, lanes)
    picked = []
    for side in range(2):
        part = spectra[side * GROUP : (side + 1) * GROUP]
        picked += [jnp.where(freq == index[side * TOPK + j], part, 0.0) for j in range(TOPK)]
    return blended, index, picked


def fetch(pairs, sems):
    copies = [pltpu.make_async_copy(a, b, sems.at[i]) for i, (a, b) in enumerate(pairs)]
    for copy in copies:
        copy.start()
    return copies


def send_kernel(
    tokens, momentum, gradient, indices, table, send, c0, c1, c2, c3, cut, mom, grad, ind, tab, sems
):
    x = lax.axis_index("shard") % XS
    piece = cut.shape[2]
    loads = fetch([(momentum, mom), (gradient, grad), (indices, ind), (table, tab)], sems)
    pieces, first = [], len(loads)
    for d in range(XS):
        for h in range(2):
            at = pl.multiple_of((h * XS + (x + d) % XS) * piece, 128)
            pieces.append((tokens.at[:, pl.ds(at, piece)], cut.at[2 * d + h]))
    cuts = fetch(pieces, sems.at[pl.ds(first, MEMBERS)])
    for load in loads:
        load.wait()
    _, index, picked = choose(mom[0], grad[0], ind, tab[...])
    values = [jnp.sum(p, axis=0, keepdims=True) for p in picked]
    message = jnp.concatenate(values + index, axis=0).astype(BF16)
    half = message.shape[1] // 2
    for r in range(send.shape[0]):
        send[r] = message[:, r % 2 * half : (r % 2 + 1) * half]
    for c in cuts:
        c.wait()
    outs = fetch(
        [(cut.at[pl.ds(2 * d, 2)], c) for d, c in enumerate((c0, c1, c2, c3))], sems.at[pl.ds(first + MEMBERS, XS)]
    )
    for out in outs:
        out.wait()


def remain_kernel(momentum, gradient, indices, table, new_momentum, mom, grad, ind, tab, sems):
    for load in fetch([(momentum, mom), (gradient, grad), (indices, ind), (table, tab)], sems):
        load.wait()
    rows = mom.shape[1]
    blended, _, picked = choose(mom[0], grad[0], ind, tab[...])
    kept = [sum(picked[side * TOPK + 1 : (side + 1) * TOPK], picked[side * TOPK]) for side in range(2)]
    field = contract(jnp.concatenate(kept, axis=0), tab[...], 0, 0)
    for p in range(blended.shape[1] // PAIR):
        at = slice(p * PAIR, (p + 1) * PAIR)
        new_momentum[0, :, at] = blended[:, at] - field[p * rows : (p + 1) * rows]


def renew_kernel(received, weight, table, renewed):
    replicas, _, lanes = received.shape
    rows = weight.shape[0]
    half = weight.shape[1] // 2
    core = lax.axis_index("replica") % 2
    freq = lax.broadcasted_iota(jnp.int32, (GROUP, 128), 0).astype(F32)
    columns = []
    for c in range(lanes // 128):
        at = slice(c * 128, (c + 1) * 128)
        sums = [jnp.zeros((GROUP, 128), F32) for _ in range(2)]
        for r in range(replicas):
            message = received[r, :, at].astype(F32)
            for side in range(2):
                for j in range(TOPK):
                    row = side * TOPK + j
                    sums[side] = sums[side] + jnp.where(
                        freq == message[8 + row][None, :], message[row][None, :], 0.0
                    )
        columns.append(jnp.concatenate(sums, axis=0))
    field = contract(jnp.concatenate(columns, axis=1), table[...], 0, 0)
    old = weight[:, pl.ds(pl.multiple_of(core * half, 128), half)].astype(F32)
    per = half // XS // PAIR
    for x in range(XS):
        for p in range(per):
            q = x * per + p
            new = old[:, q * PAIR : (q + 1) * PAIR] - STEP * field[q * rows : (q + 1) * rows]
            new = new.astype(BF16)
            for y in range(YS):
                renewed[y * XS + x, :, p * PAIR : (p + 1) * PAIR] = new


def product_kernel(t0, t1, t2, t3, came, window, mine, other):
    core = lax.axis_index("replica") % 2
    count = came.shape[1]
    for d, tokens in enumerate((t0, t1, t2, t3)):
        block = jnp.concatenate([came[d], tokens[core]], axis=0)
        product = lax.dot_general(block, window[...], (((1,), (1,)), ((), ())), preferred_element_type=F32)
        other[d] = product[:count].astype(BF16)
        mine[d] = product[count:]


def order_kernel(mine, arrived, out):
    x = lax.axis_index("shard") % XS
    for d in range(XS):
        out[(x + XS - d) % XS] = (mine[d] + arrived[d].astype(F32)).astype(BF16)


def finish_kernel(parts, out):
    total = parts[0].astype(F32)
    for x in range(1, XS):
        total = total + parts[x].astype(F32)
    out[...] = total.astype(BF16)


def call(kernel, out, *args, flops=0):
    out_list = jax.tree.leaves(out)
    moved = sum(a.size * a.dtype.itemsize for a in args) + sum(o.size * o.dtype.itemsize for o in out_list)
    return pl.pallas_call(
        kernel,
        out_shape=out,
        in_specs=[pl.BlockSpec(memory_space=pltpu.VMEM)] * len(args),
        out_specs=jax.tree.map(lambda _: pl.BlockSpec(memory_space=pltpu.VMEM), out),
        compiler_params=pltpu.CompilerParams(vmem_limit_bytes=20 * 1024 * 1024),
        cost_estimate=pl.CostEstimate(flops=flops, bytes_accessed=moved, transcendentals=0),
    )(*args)


def local(tokens, weight, momentum, gradient, indices):
    count, width = tokens.shape
    rows = weight.shape[0]
    half, piece = width // 2, width // 2 // XS
    table = jnp.asarray(pair_table())
    replicas = lax.axis_size("replica")
    shards = lax.axis_size("shard")

    lanes = width // PAIR * rows
    ordered_indices = indices[0].transpose(0, 2, 1)
    local_scratch = [
        pltpu.VMEM(momentum.shape, F32),
        pltpu.VMEM(gradient.shape, BF16),
        pltpu.VMEM(ordered_indices.shape, jnp.int32),
        pltpu.VMEM(table.shape, F32),
    ]
    hbm, vmem = pl.BlockSpec(memory_space=pltpu.HBM), pl.BlockSpec(memory_space=pltpu.VMEM)
    params = pltpu.CompilerParams(vmem_limit_bytes=VMEM_BYTES)
    with jax.named_scope("coefficients"):
        send, *cut = pl.pallas_call(
            send_kernel,
            out_shape=[jax.ShapeDtypeStruct((replicas, 4 * TOPK, lanes // 2), BF16)]
            + [jax.ShapeDtypeStruct((2, count, piece), BF16)] * XS,
            in_specs=[hbm] * 5,
            out_specs=[vmem] + [hbm] * XS,
            scratch_shapes=[pltpu.VMEM((MEMBERS, count, piece), BF16)]
            + local_scratch
            + [pltpu.SemaphoreType.DMA((4 + MEMBERS + XS,))],
            compiler_params=params,
            cost_estimate=pl.CostEstimate(flops=10**8, bytes_accessed=4 * 10**6, transcendentals=0),
        )(tokens, momentum, gradient, ordered_indices, table)

    with jax.named_scope("exchange"):
        received = lax.all_to_all(send, "replica", 0, 0)
    with jax.named_scope("renew"):
        renewed = call(
            renew_kernel, jax.ShapeDtypeStruct((shards, rows, piece), BF16), received, weight, table, flops=10**10
        )
    with jax.named_scope("momentum"):
        momentum, renewed = lax.optimization_barrier((momentum, renewed))
        new_momentum = pl.pallas_call(
            remain_kernel,
            out_shape=jax.ShapeDtypeStruct(momentum.shape, F32),
            in_specs=[hbm] * 4,
            out_specs=vmem,
            scratch_shapes=local_scratch + [pltpu.SemaphoreType.DMA((4,))],
            compiler_params=params,
            cost_estimate=pl.CostEstimate(flops=5 * 10**10, bytes_accessed=10**6, transcendentals=0),
        )(momentum, gradient, ordered_indices, table)
    with jax.named_scope("tokens_x"):
        blocks = [cut[0]] + [
            lax.ppermute(cut[d], "shard", [(s, s // XS * XS + (s + d) % XS) for s in range(shards)])
            for d in range(1, XS)
        ]
    with jax.named_scope("tokens_core"):
        away = call(swap_kernel, jax.ShapeDtypeStruct((XS, count, piece), BF16), *blocks, flops=5 * 10**10)
        came = lax.ppermute(away, "replica", [(i, i ^ 1) for i in range(replicas)])
    with jax.named_scope("window"):
        window = lax.all_to_all(renewed, "shard", 0, 0).reshape(shards * rows, piece)
    with jax.named_scope("product"):
        shape = (XS, count, shards * rows)
        mine, other = call(
            product_kernel,
            (jax.ShapeDtypeStruct(shape, F32), jax.ShapeDtypeStruct(shape, BF16)),
            *blocks,
            came,
            window,
            flops=2 * 1024 * 768 * 512,
        )
    with jax.named_scope("sum_core"):
        arrived = lax.ppermute(other, "replica", [(i, i ^ 1) for i in range(replicas)])
        ordered = call(order_kernel, jax.ShapeDtypeStruct(shape, BF16), mine, arrived)
    with jax.named_scope("sum_x"):
        groups = [[y * XS + i for i in range(XS)] for y in range(YS)]
        parts = lax.all_to_all(ordered, "shard", 0, 0, axis_index_groups=groups)
        projected = call(finish_kernel, jax.ShapeDtypeStruct(shape[1:], BF16), parts)
    return projected, new_momentum


def solution(mesh):
    in_specs = (
        P(("shard", "replica"), None),
        P("shard", None),
        P("replica", "shard", None),
        P("replica", "shard", None),
        P("replica", "shard", None, None),
    )
    out_specs = (P(("shard", "replica"), None), P("replica", "shard", None))
    return jax.shard_map(local, mesh=mesh, in_specs=in_specs, out_specs=out_specs, check_vma=False)
```

```python
import numpy as np

import jax
import jax.numpy as jnp
from jax import lax
from jax.experimental import pallas as pl
from jax.experimental.pallas import tpu as pltpu
from jax.sharding import PartitionSpec as P

GROUP = 64
TOPK = 4
DECAY = 0.999
STEP = 0.01
PAIR = 2 * GROUP
XS = 4
YS = 8
MEMBERS = 2 * XS
VMEM_BYTES = 60 * 1024 * 1024
F32 = jnp.float32
BF16 = jnp.bfloat16
HIGH = lax.Precision.HIGHEST


def pair_table():
    k = np.arange(GROUP, dtype=np.float64)[:, None]
    n = np.arange(GROUP, dtype=np.float64)[None, :]
    c = np.cos(np.pi * (2.0 * n + 1.0) * k / (2.0 * GROUP)) * np.sqrt(2.0 / GROUP)
    c = c * np.where(k == 0, np.sqrt(0.5), 1.0)
    both = np.zeros((PAIR, PAIR), np.float64)
    both[:GROUP, :GROUP] = c
    both[GROUP:, GROUP:] = c
    return both.astype(np.float32)


def contract(a, b, da, db):
    return lax.dot_general(a, b, (((da,), (db,)), ((), ())), precision=HIGH, preferred_element_type=F32)


def forward_kernel(ahead, behind, far0, far1):
    far0[0] = ahead[2]
    far1[0] = behind[2]


def lay_out(indices, lanes):
    rows, _, groups = indices.shape
    spread = lax.broadcasted_iota(jnp.int32, (rows, lanes), 1) % rows
    spread = jnp.where(spread == lax.broadcasted_iota(jnp.int32, (rows, lanes), 0), 1.0, 0.0).astype(BF16)
    pair = lax.broadcasted_iota(jnp.int32, (groups, lanes), 1) // rows
    transform = lax.broadcasted_iota(jnp.int32, (groups, lanes), 0)
    spreads = [
        lax.dot_general(
            indices[:, j, :].astype(F32).astype(BF16), spread, (((0,), (0,)), ((), ())), preferred_element_type=F32
        )
        for j in range(TOPK)
    ]
    return [
        jnp.sum(jnp.where(transform == 2 * pair + side, spreads[j], 0.0), axis=0, keepdims=True)
        for side in range(2)
        for j in range(TOPK)
    ]


def choose(momentum, gradient, indices, table):
    rows, width = momentum.shape
    pairs = width // PAIR
    lanes = pairs * rows
    blended = DECAY * momentum + gradient.astype(F32)
    stacked = jnp.concatenate([blended[:, p * PAIR : (p + 1) * PAIR] for p in range(pairs)], axis=0)
    spectra = contract(table, stacked, 1, 1)
    freq = lax.broadcasted_iota(jnp.int32, (GROUP, lanes), 0).astype(F32)
    index = lay_out(indices, lanes)
    picked = []
    for side in range(2):
        part = spectra[side * GROUP : (side + 1) * GROUP]
        picked += [jnp.where(freq == index[side * TOPK + j], part, 0.0) for j in range(TOPK)]
    return blended, index, picked


def fetch(pairs, sems):
    copies = [pltpu.make_async_copy(a, b, sems.at[i]) for i, (a, b) in enumerate(pairs)]
    for copy in copies:
        copy.start()
    return copies


def send_kernel(
    tokens, momentum, gradient, indices, table, send, own, ahead, behind, cut, mom, grad, ind, tab, sems
):
    x = lax.axis_index("shard") % XS
    piece = cut.shape[2]
    loads = fetch([(momentum, mom), (gradient, grad), (indices, ind), (table, tab)], sems)
    pieces, first = [], len(loads)
    for i, (d, h) in enumerate([(0, 0), (0, 1), (1, 0), (1, 1), (2, 0), (3, 0), (3, 1), (2, 1)]):
        at = pl.multiple_of((h * XS + (x + d) % XS) * piece, 128)
        pieces.append((tokens.at[:, pl.ds(at, piece)], cut.at[i]))
    cuts = fetch(pieces, sems.at[pl.ds(first, MEMBERS)])
    for c in cuts:
        c.wait()
    outs = fetch(
        [(cut.at[pl.ds(0, 2)], own), (cut.at[pl.ds(2, 3)], ahead), (cut.at[pl.ds(5, 3)], behind)],
        sems.at[pl.ds(first + MEMBERS, 3)],
    )
    for load in loads:
        load.wait()
    _, index, picked = choose(mom[0], grad[0], ind, tab[...])
    values = [jnp.sum(p, axis=0, keepdims=True) for p in picked]
    message = jnp.concatenate(values + index, axis=0).astype(BF16)
    half = message.shape[1] // 2
    for r in range(send.shape[0]):
        send[r] = message[:, r % 2 * half : (r % 2 + 1) * half]
    for out in outs:
        out.wait()


def remain_kernel(momentum, gradient, indices, table, new_momentum, mom, grad, ind, tab, sems):
    for load in fetch([(momentum, mom), (gradient, grad), (indices, ind), (table, tab)], sems):
        load.wait()
    rows = mom.shape[1]
    blended, _, picked = choose(mom[0], grad[0], ind, tab[...])
    kept = [sum(picked[side * TOPK + 1 : (side + 1) * TOPK], picked[side * TOPK]) for side in range(2)]
    field = contract(jnp.concatenate(kept, axis=0), tab[...], 0, 0)
    for p in range(blended.shape[1] // PAIR):
        at = slice(p * PAIR, (p + 1) * PAIR)
        new_momentum[0, :, at] = blended[:, at] - field[p * rows : (p + 1) * rows]


def renew_kernel(received, weight, table, renewed):
    replicas, _, lanes = received.shape
    rows = weight.shape[0]
    half = weight.shape[1] // 2
    core = lax.axis_index("replica") % 2
    freq = lax.broadcasted_iota(jnp.int32, (GROUP, 128), 0).astype(F32)
    columns = []
    for c in range(lanes // 128):
        at = slice(c * 128, (c + 1) * 128)
        sums = [jnp.zeros((GROUP, 128), F32) for _ in range(2)]
        for r in range(replicas):
            message = received[r, :, at].astype(F32)
            for side in range(2):
                dense = jnp.zeros((GROUP, 128), F32)
                for row in range(side * TOPK, (side + 1) * TOPK):
                    dense = jnp.where(freq == message[2 * TOPK + row][None, :], message[row][None, :], dense)
                sums[side] = sums[side] + dense
        columns.append(jnp.concatenate(sums, axis=0))
    field = contract(jnp.concatenate(columns, axis=1), table[...], 0, 0)
    old = weight[:, pl.ds(pl.multiple_of(core * half, 128), half)].astype(F32)
    per = half // XS // PAIR
    for x in range(XS):
        for p in range(per):
            q = x * per + p
            new = old[:, q * PAIR : (q + 1) * PAIR] - STEP * field[q * rows : (q + 1) * rows]
            new = new.astype(BF16)
            for y in range(YS):
                renewed[y * XS + x, :, p * PAIR : (p + 1) * PAIR] = new


def stack(own, ahead, far0, far1, behind, h):
    return jnp.concatenate([own[h], ahead[h], jnp.where(h == 0, far0[0], far1[0]), behind[h]], axis=0)


def product(tokens, window):
    return lax.dot_general(tokens, window[...], (((1,), (1,)), ((), ())), preferred_element_type=F32)


def first_kernel(*refs):
    *blocks, window, out = refs
    out[...] = product(stack(*blocks, lax.axis_index("replica") % 2), window)


def second_kernel(*refs):
    *blocks, window, first, out = refs
    x = lax.axis_index("shard") % XS
    count = out.shape[1]
    total = first[...] + product(stack(*blocks, 1 - lax.axis_index("replica") % 2), window)
    for d in range(XS):
        out[(x + XS - d) % XS] = total[d * count : (d + 1) * count].astype(BF16)


def finish_kernel(parts, out):
    total = parts[0].astype(F32)
    for x in range(1, XS):
        total = total + parts[x].astype(F32)
    out[...] = total.astype(BF16)


def call(kernel, out, *args, flops=0):
    out_list = jax.tree.leaves(out)
    moved = sum(a.size * a.dtype.itemsize for a in args) + sum(o.size * o.dtype.itemsize for o in out_list)
    return pl.pallas_call(
        kernel,
        out_shape=out,
        in_specs=[pl.BlockSpec(memory_space=pltpu.VMEM)] * len(args),
        out_specs=jax.tree.map(lambda _: pl.BlockSpec(memory_space=pltpu.VMEM), out),
        compiler_params=pltpu.CompilerParams(vmem_limit_bytes=20 * 1024 * 1024),
        cost_estimate=pl.CostEstimate(flops=flops, bytes_accessed=moved, transcendentals=0),
    )(*args)


def local(tokens, weight, momentum, gradient, indices):
    count, width = tokens.shape
    rows = weight.shape[0]
    half, piece = width // 2, width // 2 // XS
    table = jnp.asarray(pair_table())
    replicas = lax.axis_size("replica")
    shards = lax.axis_size("shard")

    lanes = width // PAIR * rows
    ordered_indices = indices[0].transpose(0, 2, 1)
    local_scratch = [
        pltpu.VMEM(momentum.shape, F32),
        pltpu.VMEM(gradient.shape, BF16),
        pltpu.VMEM(ordered_indices.shape, jnp.int32),
        pltpu.VMEM(table.shape, F32),
    ]
    hbm, vmem = pl.BlockSpec(memory_space=pltpu.HBM), pl.BlockSpec(memory_space=pltpu.VMEM)
    params = pltpu.CompilerParams(vmem_limit_bytes=VMEM_BYTES)
    with jax.named_scope("coefficients"):
        send, own, ahead, behind = pl.pallas_call(
            send_kernel,
            out_shape=[jax.ShapeDtypeStruct((replicas, 4 * TOPK, lanes // 2), BF16)]
            + [jax.ShapeDtypeStruct((n, count, piece), BF16) for n in (2, 3, 3)],
            in_specs=[hbm] * 5,
            out_specs=[vmem] + [hbm] * 3,
            scratch_shapes=[pltpu.VMEM((MEMBERS, count, piece), BF16)]
            + local_scratch
            + [pltpu.SemaphoreType.DMA((4 + MEMBERS + 3,))],
            compiler_params=params,
            cost_estimate=pl.CostEstimate(flops=10**8, bytes_accessed=4 * 10**6, transcendentals=0),
        )(tokens, momentum, gradient, ordered_indices, table)

    with jax.named_scope("exchange"):
        received = lax.all_to_all(send, "replica", 0, 0)
    with jax.named_scope("renew"):
        renewed = call(
            renew_kernel, jax.ShapeDtypeStruct((shards, rows, piece), BF16), received, weight, table, flops=10**10
        )
    with jax.named_scope("tokens_x"):
        on, back = (
            [(s, s // XS * XS + (s + step) % XS) for s in range(shards)] for step in (1, XS - 1)
        )
        ahead = lax.ppermute(ahead, "shard", on)
        behind = lax.ppermute(behind, "shard", back)
        one = jax.ShapeDtypeStruct((1, count, piece), BF16)
        far0, far1 = call(forward_kernel, [one, one], ahead, behind, flops=5 * 10**10)
        far0 = lax.ppermute(far0, "shard", on)
        far1 = lax.ppermute(far1, "shard", back)
        blocks = (own, ahead, far0, far1, behind)
    with jax.named_scope("momentum"):
        momentum, renewed = lax.optimization_barrier((momentum, renewed))
        new_momentum = pl.pallas_call(
            remain_kernel,
            out_shape=jax.ShapeDtypeStruct(momentum.shape, F32),
            in_specs=[hbm] * 4,
            out_specs=vmem,
            scratch_shapes=local_scratch + [pltpu.SemaphoreType.DMA((4,))],
            compiler_params=params,
            cost_estimate=pl.CostEstimate(flops=5 * 10**10, bytes_accessed=10**6, transcendentals=0),
        )(momentum, gradient, ordered_indices, table)
    with jax.named_scope("window"):
        window = lax.all_to_all(renewed, "shard", 0, 0).reshape(shards * rows, piece)
    with jax.named_scope("window_core"):
        window, *blocks = lax.optimization_barrier((window, *blocks))
        other = lax.ppermute(window, "replica", [(i, i ^ 1) for i in range(replicas)])
    with jax.named_scope("product"):
        size = shards * rows
        work = 2 * XS * count * size * piece
        first = call(first_kernel, jax.ShapeDtypeStruct((XS * count, size), F32), *blocks, window, flops=work)
        shape = (XS, count, size)
        ordered = call(second_kernel, jax.ShapeDtypeStruct(shape, BF16), *blocks, other, first, flops=work)
    with jax.named_scope("sum_x"):
        groups = [[y * XS + i for i in range(XS)] for y in range(YS)]
        parts = lax.all_to_all(ordered, "shard", 0, 0, axis_index_groups=groups)
        projected = call(finish_kernel, jax.ShapeDtypeStruct(shape[1:], BF16), parts)
    return projected, new_momentum


def solution(mesh):
    in_specs = (
        P(("shard", "replica"), None),
        P("shard", None),
        P("replica", "shard", None),
        P("replica", "shard", None),
        P("replica", "shard", None, None),
    )
    out_specs = (P(("shard", "replica"), None), P("replica", "shard", None))
    return jax.shard_map(local, mesh=mesh, in_specs=in_specs, out_specs=out_specs, check_vma=False)
```

```python
import numpy as np

import jax
import jax.numpy as jnp
from jax import lax
from jax.experimental import pallas as pl
from jax.experimental.pallas import tpu as pltpu
from jax.sharding import PartitionSpec as P

GROUP = 64
TOPK = 4
DECAY = 0.999
STEP = 0.01
PAIR = 2 * GROUP
XS = 4
YS = 8
MEMBERS = 2 * XS
VMEM_BYTES = 60 * 1024 * 1024
F32 = jnp.float32
BF16 = jnp.bfloat16
HIGH = lax.Precision.HIGHEST


def pair_table():
    k = np.arange(GROUP, dtype=np.float64)[:, None]
    n = np.arange(GROUP, dtype=np.float64)[None, :]
    c = np.cos(np.pi * (2.0 * n + 1.0) * k / (2.0 * GROUP)) * np.sqrt(2.0 / GROUP)
    c = c * np.where(k == 0, np.sqrt(0.5), 1.0)
    both = np.zeros((PAIR, PAIR), np.float64)
    both[:GROUP, :GROUP] = c
    both[GROUP:, GROUP:] = c
    return both.astype(np.float32)


def contract(a, b, da, db):
    return lax.dot_general(a, b, (((da,), (db,)), ((), ())), precision=HIGH, preferred_element_type=F32)


def forward_kernel(ahead, behind, far0, far1):
    far0[0] = ahead[2]
    far1[0] = behind[2]


def lay_out(indices, lanes):
    rows, _, groups = indices.shape
    spread = lax.broadcasted_iota(jnp.int32, (rows, lanes), 1) % rows
    spread = jnp.where(spread == lax.broadcasted_iota(jnp.int32, (rows, lanes), 0), 1.0, 0.0).astype(BF16)
    pair = lax.broadcasted_iota(jnp.int32, (groups, lanes), 1) // rows
    transform = lax.broadcasted_iota(jnp.int32, (groups, lanes), 0)
    spreads = [
        lax.dot_general(
            indices[:, j, :].astype(F32).astype(BF16), spread, (((0,), (0,)), ((), ())), preferred_element_type=F32
        )
        for j in range(TOPK)
    ]
    return [
        jnp.sum(jnp.where(transform == 2 * pair + side, spreads[j], 0.0), axis=0, keepdims=True)
        for side in range(2)
        for j in range(TOPK)
    ]


def choose(momentum, gradient, indices, table):
    rows, width = momentum.shape
    pairs = width // PAIR
    lanes = pairs * rows
    blended = DECAY * momentum + gradient.astype(F32)
    stacked = jnp.concatenate([blended[:, p * PAIR : (p + 1) * PAIR] for p in range(pairs)], axis=0)
    spectra = contract(table, stacked, 1, 1)
    freq = lax.broadcasted_iota(jnp.int32, (GROUP, lanes), 0).astype(F32)
    index = lay_out(indices, lanes)
    picked = []
    for side in range(2):
        part = spectra[side * GROUP : (side + 1) * GROUP]
        picked += [jnp.where(freq == index[side * TOPK + j], part, 0.0) for j in range(TOPK)]
    return blended, index, picked


def fetch(pairs, sems):
    copies = [pltpu.make_async_copy(a, b, sems.at[i]) for i, (a, b) in enumerate(pairs)]
    for copy in copies:
        copy.start()
    return copies


def send_kernel(momentum, gradient, indices, table, send, mom, grad, ind, tab, sems):
    for load in fetch([(momentum, mom), (gradient, grad), (indices, ind), (table, tab)], sems):
        load.wait()
    _, index, picked = choose(mom[0], grad[0], ind, tab[...])
    values = [jnp.sum(p, axis=0, keepdims=True) for p in picked]
    message = jnp.concatenate(values + index, axis=0).astype(BF16)
    half = message.shape[1] // 2
    for r in range(send.shape[0]):
        send[r] = message[:, r % 2 * half : (r % 2 + 1) * half]


def cut_kernel(tokens, own, ahead, behind, cut, sems):
    x = lax.axis_index("shard") % XS
    piece = cut.shape[2]
    pieces = []
    for i, (d, h) in enumerate([(1, 0), (1, 1), (2, 0), (3, 0), (3, 1), (2, 1), (0, 0), (0, 1)]):
        at = pl.multiple_of((h * XS + (x + d) % XS) * piece, 128)
        pieces.append((tokens.at[:, pl.ds(at, piece)], cut.at[i]))
    cuts = fetch(pieces, sems)
    outs = []
    for i, (first, number, out) in enumerate([(0, 3, ahead), (3, 3, behind), (6, 2, own)]):
        for c in cuts[first : first + number]:
            c.wait()
        outs += fetch([(cut.at[pl.ds(first, number)], out)], sems.at[pl.ds(MEMBERS + i, 1)])
    for out in outs:
        out.wait()


def remain_kernel(momentum, gradient, indices, table, new_momentum, mom, grad, ind, tab, sems):
    for load in fetch([(momentum, mom), (gradient, grad), (indices, ind), (table, tab)], sems):
        load.wait()
    rows = mom.shape[1]
    blended, _, picked = choose(mom[0], grad[0], ind, tab[...])
    kept = [sum(picked[side * TOPK + 1 : (side + 1) * TOPK], picked[side * TOPK]) for side in range(2)]
    field = contract(jnp.concatenate(kept, axis=0), tab[...], 0, 0)
    for p in range(blended.shape[1] // PAIR):
        at = slice(p * PAIR, (p + 1) * PAIR)
        new_momentum[0, :, at] = blended[:, at] - field[p * rows : (p + 1) * rows]


def renew_kernel(received, weight, table, renewed):
    replicas, _, lanes = received.shape
    rows = weight.shape[0]
    half = weight.shape[1] // 2
    core = lax.axis_index("replica") % 2
    freq = lax.broadcasted_iota(jnp.int32, (GROUP, 128), 0).astype(F32)
    columns = []
    for c in range(lanes // 128):
        at = slice(c * 128, (c + 1) * 128)
        sums = [jnp.zeros((GROUP, 128), F32) for _ in range(2)]
        for r in range(replicas):
            message = received[r, :, at].astype(F32)
            for side in range(2):
                dense = jnp.zeros((GROUP, 128), F32)
                for row in range(side * TOPK, (side + 1) * TOPK):
                    dense = jnp.where(freq == message[2 * TOPK + row][None, :], message[row][None, :], dense)
                sums[side] = sums[side] + dense
        columns.append(jnp.concatenate(sums, axis=0))
    field = contract(jnp.concatenate(columns, axis=1), table[...], 0, 0)
    old = weight[:, pl.ds(pl.multiple_of(core * half, 128), half)].astype(F32)
    per = half // XS // PAIR
    for x in range(XS):
        for p in range(per):
            q = x * per + p
            new = old[:, q * PAIR : (q + 1) * PAIR] - STEP * field[q * rows : (q + 1) * rows]
            new = new.astype(BF16)
            for y in range(YS):
                renewed[y * XS + x, :, p * PAIR : (p + 1) * PAIR] = new


def stack(own, ahead, far0, far1, behind, h):
    return jnp.concatenate([own[h], ahead[h], jnp.where(h == 0, far0[0], far1[0]), behind[h]], axis=0)


def product(tokens, window):
    return lax.dot_general(tokens, window[...], (((1,), (1,)), ((), ())), preferred_element_type=F32)


def first_kernel(*refs):
    *blocks, window, out, rest = refs
    core = lax.axis_index("replica") % 2
    out[...] = product(stack(*blocks, core), window)
    rest[...] = stack(*blocks, 1 - core)


def second_kernel(rest, window, first, out):
    x = lax.axis_index("shard") % XS
    count = out.shape[1]
    total = first[...] + product(rest[...], window)
    for d in range(XS):
        out[(x + XS - d) % XS] = total[d * count : (d + 1) * count].astype(BF16)


def finish_kernel(parts, out):
    total = parts[0].astype(F32)
    for x in range(1, XS):
        total = total + parts[x].astype(F32)
    out[...] = total.astype(BF16)


def call(kernel, out, *args, flops=0):
    out_list = jax.tree.leaves(out)
    moved = sum(a.size * a.dtype.itemsize for a in args) + sum(o.size * o.dtype.itemsize for o in out_list)
    return pl.pallas_call(
        kernel,
        out_shape=out,
        in_specs=[pl.BlockSpec(memory_space=pltpu.VMEM)] * len(args),
        out_specs=jax.tree.map(lambda _: pl.BlockSpec(memory_space=pltpu.VMEM), out),
        compiler_params=pltpu.CompilerParams(vmem_limit_bytes=20 * 1024 * 1024),
        cost_estimate=pl.CostEstimate(flops=flops, bytes_accessed=moved, transcendentals=0),
    )(*args)


def local(tokens, weight, momentum, gradient, indices):
    count, width = tokens.shape
    rows = weight.shape[0]
    half, piece = width // 2, width // 2 // XS
    table = jnp.asarray(pair_table())
    replicas = lax.axis_size("replica")
    shards = lax.axis_size("shard")

    lanes = width // PAIR * rows
    ordered_indices = indices[0].transpose(0, 2, 1)
    local_scratch = [
        pltpu.VMEM(momentum.shape, F32),
        pltpu.VMEM(gradient.shape, BF16),
        pltpu.VMEM(ordered_indices.shape, jnp.int32),
        pltpu.VMEM(table.shape, F32),
    ]
    hbm, vmem = pl.BlockSpec(memory_space=pltpu.HBM), pl.BlockSpec(memory_space=pltpu.VMEM)
    params = pltpu.CompilerParams(vmem_limit_bytes=VMEM_BYTES)
    with jax.named_scope("coefficients"):
        send = pl.pallas_call(
            send_kernel,
            out_shape=jax.ShapeDtypeStruct((replicas, 4 * TOPK, lanes // 2), BF16),
            in_specs=[hbm] * 4,
            out_specs=vmem,
            scratch_shapes=local_scratch + [pltpu.SemaphoreType.DMA((4,))],
            compiler_params=params,
            cost_estimate=pl.CostEstimate(flops=10**8, bytes_accessed=10**6, transcendentals=0),
        )(momentum, gradient, ordered_indices, table)
    with jax.named_scope("cut"):
        tokens, send = lax.optimization_barrier((tokens, send))
        own, ahead, behind = pl.pallas_call(
            cut_kernel,
            out_shape=[jax.ShapeDtypeStruct((n, count, piece), BF16) for n in (2, 3, 3)],
            in_specs=[hbm],
            out_specs=[hbm] * 3,
            scratch_shapes=[pltpu.VMEM((MEMBERS, count, piece), BF16), pltpu.SemaphoreType.DMA((MEMBERS + 3,))],
            compiler_params=params,
            cost_estimate=pl.CostEstimate(flops=0, bytes_accessed=4 * tokens.size, transcendentals=0),
        )(tokens)

    with jax.named_scope("exchange"):
        received = lax.all_to_all(send, "replica", 0, 0)
    with jax.named_scope("renew"):
        renewed = call(
            renew_kernel, jax.ShapeDtypeStruct((shards, rows, piece), BF16), received, weight, table, flops=10**10
        )
    with jax.named_scope("tokens_x"):
        on, back = (
            [(s, s // XS * XS + (s + step) % XS) for s in range(shards)] for step in (1, XS - 1)
        )
        ahead = lax.ppermute(ahead, "shard", on)
        behind = lax.ppermute(behind, "shard", back)
        one = jax.ShapeDtypeStruct((1, count, piece), BF16)
        far0, far1 = call(forward_kernel, [one, one], ahead, behind, flops=5 * 10**10)
        far0 = lax.ppermute(far0, "shard", on)
        far1 = lax.ppermute(far1, "shard", back)
        blocks = (own, ahead, far0, far1, behind)
    with jax.named_scope("momentum"):
        momentum, renewed = lax.optimization_barrier((momentum, renewed))
        new_momentum = pl.pallas_call(
            remain_kernel,
            out_shape=jax.ShapeDtypeStruct(momentum.shape, F32),
            in_specs=[hbm] * 4,
            out_specs=vmem,
            scratch_shapes=local_scratch + [pltpu.SemaphoreType.DMA((4,))],
            compiler_params=params,
            cost_estimate=pl.CostEstimate(flops=5 * 10**10, bytes_accessed=10**6, transcendentals=0),
        )(momentum, gradient, ordered_indices, table)
    with jax.named_scope("window"):
        window = lax.all_to_all(renewed, "shard", 0, 0).reshape(shards * rows, piece)
    with jax.named_scope("window_core"):
        window, *blocks = lax.optimization_barrier((window, *blocks))
        other = lax.ppermute(window, "replica", [(i, i ^ 1) for i in range(replicas)])
    with jax.named_scope("product"):
        size = shards * rows
        work = 2 * XS * count * size * piece
        first, rest = call(
            first_kernel,
            [
                jax.ShapeDtypeStruct((XS * count, size), F32),
                jax.ShapeDtypeStruct((XS * count, piece), BF16),
            ],
            *blocks,
            window,
            flops=work,
        )
        shape = (XS, count, size)
        ordered = call(second_kernel, jax.ShapeDtypeStruct(shape, BF16), rest, other, first, flops=work)
    with jax.named_scope("sum_x"):
        groups = [[y * XS + i for i in range(XS)] for y in range(YS)]
        parts = lax.all_to_all(ordered, "shard", 0, 0, axis_index_groups=groups)
        projected = call(finish_kernel, jax.ShapeDtypeStruct(shape[1:], BF16), parts)
    return projected, new_momentum


def solution(mesh):
    in_specs = (
        P(("shard", "replica"), None),
        P("shard", None),
        P("replica", "shard", None),
        P("replica", "shard", None),
        P("replica", "shard", None, None),
    )
    out_specs = (P(("shard", "replica"), None), P("replica", "shard", None))
    return jax.shard_map(local, mesh=mesh, in_specs=in_specs, out_specs=out_specs, check_vma=False)
```

```python
import numpy as np

import jax
import jax.numpy as jnp
from jax import lax
from jax.experimental import pallas as pl
from jax.experimental.pallas import tpu as pltpu
from jax.sharding import PartitionSpec as P

GROUP = 64
TOPK = 4
DECAY = 0.999
STEP = 0.01
PAIR = 2 * GROUP
XS = 4
YS = 8
MEMBERS = 2 * XS
VMEM_BYTES = 60 * 1024 * 1024
F32 = jnp.float32
BF16 = jnp.bfloat16
HIGH = lax.Precision.HIGHEST


def pair_table():
    k = np.arange(GROUP, dtype=np.float64)[:, None]
    n = np.arange(GROUP, dtype=np.float64)[None, :]
    c = np.cos(np.pi * (2.0 * n + 1.0) * k / (2.0 * GROUP)) * np.sqrt(2.0 / GROUP)
    c = c * np.where(k == 0, np.sqrt(0.5), 1.0)
    both = np.zeros((PAIR, PAIR), np.float64)
    both[:GROUP, :GROUP] = c
    both[GROUP:, GROUP:] = c
    return both.astype(np.float32)


def contract(a, b, da, db):
    return lax.dot_general(a, b, (((da,), (db,)), ((), ())), precision=HIGH, preferred_element_type=F32)


def forward_kernel(ahead, behind, far0, far1):
    far0[0] = ahead[2]
    far1[0] = behind[2]


def own_kernel(tokens, own, sems):
    x = lax.axis_index("shard") % XS
    piece = own.shape[2]
    halves = [pl.multiple_of((h * XS + x) * piece, 128) for h in range(2)]
    for copy in fetch([(tokens.at[:, pl.ds(at, piece)], own.at[h]) for h, at in enumerate(halves)], sems):
        copy.wait()


def lay_out(indices, lanes):
    rows, _, groups = indices.shape
    spread = lax.broadcasted_iota(jnp.int32, (rows, lanes), 1) % rows
    spread = jnp.where(spread == lax.broadcasted_iota(jnp.int32, (rows, lanes), 0), 1.0, 0.0).astype(BF16)
    pair = lax.broadcasted_iota(jnp.int32, (groups, lanes), 1) // rows
    transform = lax.broadcasted_iota(jnp.int32, (groups, lanes), 0)
    spreads = [
        lax.dot_general(
            indices[:, j, :].astype(F32).astype(BF16), spread, (((0,), (0,)), ((), ())), preferred_element_type=F32
        )
        for j in range(TOPK)
    ]
    return [
        jnp.sum(jnp.where(transform == 2 * pair + side, spreads[j], 0.0), axis=0, keepdims=True)
        for side in range(2)
        for j in range(TOPK)
    ]


def choose(momentum, gradient, indices, table):
    rows, width = momentum.shape
    pairs = width // PAIR
    lanes = pairs * rows
    blended = DECAY * momentum + gradient.astype(F32)
    stacked = jnp.concatenate([blended[:, p * PAIR : (p + 1) * PAIR] for p in range(pairs)], axis=0)
    spectra = contract(table, stacked, 1, 1)
    freq = lax.broadcasted_iota(jnp.int32, (GROUP, lanes), 0).astype(F32)
    index = lay_out(indices, lanes)
    picked = []
    for side in range(2):
        part = spectra[side * GROUP : (side + 1) * GROUP]
        picked += [jnp.where(freq == index[side * TOPK + j], part, 0.0) for j in range(TOPK)]
    return blended, index, picked


def fetch(pairs, sems):
    copies = [pltpu.make_async_copy(a, b, sems.at[i]) for i, (a, b) in enumerate(pairs)]
    for copy in copies:
        copy.start()
    return copies


def send_kernel(momentum, gradient, indices, table, send, mom, grad, ind, tab, sems):
    for load in fetch([(momentum, mom), (gradient, grad), (indices, ind), (table, tab)], sems):
        load.wait()
    _, index, picked = choose(mom[0], grad[0], ind, tab[...])
    values = [jnp.sum(p, axis=0, keepdims=True) for p in picked]
    message = jnp.concatenate(values + index, axis=0).astype(BF16)
    half = message.shape[1] // 2
    for r in range(send.shape[0]):
        send[r] = message[:, r % 2 * half : (r % 2 + 1) * half]


def cut_kernel(tokens, ahead, behind, cut, sems):
    x = lax.axis_index("shard") % XS
    piece = cut.shape[2]
    pieces = []
    for i, (d, h) in enumerate([(1, 0), (1, 1), (2, 0), (3, 0), (3, 1), (2, 1)]):
        at = pl.multiple_of((h * XS + (x + d) % XS) * piece, 128)
        pieces.append((tokens.at[:, pl.ds(at, piece)], cut.at[i]))
    cuts = fetch(pieces, sems)
    outs = []
    for i, (first, number, out) in enumerate([(0, 3, ahead), (3, 3, behind)]):
        for c in cuts[first : first + number]:
            c.wait()
        outs += fetch([(cut.at[pl.ds(first, number)], out)], sems.at[pl.ds(len(pieces) + i, 1)])
    for out in outs:
        out.wait()


def remain_kernel(momentum, gradient, indices, table, new_momentum, mom, grad, ind, tab, sems):
    for load in fetch([(momentum, mom), (gradient, grad), (indices, ind), (table, tab)], sems):
        load.wait()
    rows = mom.shape[1]
    blended, _, picked = choose(mom[0], grad[0], ind, tab[...])
    kept = [sum(picked[side * TOPK + 1 : (side + 1) * TOPK], picked[side * TOPK]) for side in range(2)]
    field = contract(jnp.concatenate(kept, axis=0), tab[...], 0, 0)
    for p in range(blended.shape[1] // PAIR):
        at = slice(p * PAIR, (p + 1) * PAIR)
        new_momentum[0, :, at] = blended[:, at] - field[p * rows : (p + 1) * rows]


def renew_kernel(received, weight, table, renewed):
    replicas, _, lanes = received.shape
    rows = weight.shape[0]
    half = weight.shape[1] // 2
    core = lax.axis_index("replica") % 2
    freq = lax.broadcasted_iota(jnp.int32, (GROUP, 128), 0).astype(F32).astype(BF16)
    columns = []
    for c in range(lanes // 128):
        at = slice(c * 128, (c + 1) * 128)
        sums = [jnp.zeros((GROUP, 128), F32) for _ in range(2)]
        for r in range(replicas):
            message = received[r, :, at]
            for side in range(2):
                dense = jnp.zeros((GROUP, 128), BF16)
                for row in range(side * TOPK, (side + 1) * TOPK):
                    dense = jnp.where(freq == message[2 * TOPK + row][None, :], message[row][None, :], dense)
                sums[side] = sums[side] + dense.astype(F32)
        columns.append(jnp.concatenate(sums, axis=0))
    field = contract(jnp.concatenate(columns, axis=1), table[...], 0, 0)
    old = weight[:, pl.ds(pl.multiple_of(core * half, 128), half)].astype(F32)
    per = half // XS // PAIR
    for x in range(XS):
        for p in range(per):
            q = x * per + p
            new = old[:, q * PAIR : (q + 1) * PAIR] - STEP * field[q * rows : (q + 1) * rows]
            new = new.astype(BF16)
            for y in range(YS):
                renewed[y * XS + x, :, p * PAIR : (p + 1) * PAIR] = new


def stack(own, ahead, far0, far1, behind, h):
    return jnp.concatenate([own[h], ahead[h], jnp.where(h == 0, far0[0], far1[0]), behind[h]], axis=0)


def product(tokens, window):
    return lax.dot_general(tokens, window[...], (((1,), (1,)), ((), ())), preferred_element_type=F32)


def first_kernel(*refs):
    *blocks, window, out, rest = refs
    core = lax.axis_index("replica") % 2
    out[...] = product(stack(*blocks, core), window)
    rest[...] = stack(*blocks, 1 - core)


def second_kernel(rest, window, first, out):
    x = lax.axis_index("shard") % XS
    count = out.shape[1]
    total = first[...] + product(rest[...], window)
    for d in range(XS):
        out[(x + XS - d) % XS] = total[d * count : (d + 1) * count].astype(BF16)


def finish_kernel(parts, out):
    total = parts[0].astype(F32)
    for x in range(1, XS):
        total = total + parts[x].astype(F32)
    out[...] = total.astype(BF16)


def call(kernel, out, *args, flops=0):
    out_list = jax.tree.leaves(out)
    moved = sum(a.size * a.dtype.itemsize for a in args) + sum(o.size * o.dtype.itemsize for o in out_list)
    return pl.pallas_call(
        kernel,
        out_shape=out,
        in_specs=[pl.BlockSpec(memory_space=pltpu.VMEM)] * len(args),
        out_specs=jax.tree.map(lambda _: pl.BlockSpec(memory_space=pltpu.VMEM), out),
        compiler_params=pltpu.CompilerParams(vmem_limit_bytes=20 * 1024 * 1024),
        cost_estimate=pl.CostEstimate(flops=flops, bytes_accessed=moved, transcendentals=0),
    )(*args)


def local(tokens, weight, momentum, gradient, indices):
    count, width = tokens.shape
    rows = weight.shape[0]
    half, piece = width // 2, width // 2 // XS
    table = jnp.asarray(pair_table())
    replicas = lax.axis_size("replica")
    shards = lax.axis_size("shard")

    lanes = width // PAIR * rows
    ordered_indices = indices[0].transpose(0, 2, 1)
    local_scratch = [
        pltpu.VMEM(momentum.shape, F32),
        pltpu.VMEM(gradient.shape, BF16),
        pltpu.VMEM(ordered_indices.shape, jnp.int32),
        pltpu.VMEM(table.shape, F32),
    ]
    hbm, vmem = pl.BlockSpec(memory_space=pltpu.HBM), pl.BlockSpec(memory_space=pltpu.VMEM)
    params = pltpu.CompilerParams(vmem_limit_bytes=VMEM_BYTES)
    with jax.named_scope("coefficients"):
        send = pl.pallas_call(
            send_kernel,
            out_shape=jax.ShapeDtypeStruct((replicas, 4 * TOPK, lanes // 2), BF16),
            in_specs=[hbm] * 4,
            out_specs=vmem,
            scratch_shapes=local_scratch + [pltpu.SemaphoreType.DMA((4,))],
            compiler_params=params,
            cost_estimate=pl.CostEstimate(flops=10**8, bytes_accessed=10**6, transcendentals=0),
        )(momentum, gradient, ordered_indices, table)
    with jax.named_scope("cut"):
        tokens, send = lax.optimization_barrier((tokens, send))
        ahead, behind = pl.pallas_call(
            cut_kernel,
            out_shape=[jax.ShapeDtypeStruct((n, count, piece), BF16) for n in (3, 3)],
            in_specs=[hbm],
            out_specs=[hbm] * 2,
            scratch_shapes=[pltpu.VMEM((6, count, piece), BF16), pltpu.SemaphoreType.DMA((8,))],
            compiler_params=params,
            cost_estimate=pl.CostEstimate(flops=0, bytes_accessed=4 * tokens.size, transcendentals=0),
        )(tokens)

    with jax.named_scope("exchange"):
        received = lax.all_to_all(send, "replica", 0, 0)
    with jax.named_scope("renew"):
        renewed = call(
            renew_kernel, jax.ShapeDtypeStruct((shards, rows, piece), BF16), received, weight, table, flops=10**10
        )
    with jax.named_scope("tokens_x"):
        on, back = (
            [(s, s // XS * XS + (s + step) % XS) for s in range(shards)] for step in (1, XS - 1)
        )
        ahead = lax.ppermute(ahead, "shard", on)
        behind = lax.ppermute(behind, "shard", back)
        one = jax.ShapeDtypeStruct((1, count, piece), BF16)
        far0, far1 = call(forward_kernel, [one, one], ahead, behind, flops=5 * 10**10)
        far0 = lax.ppermute(far0, "shard", on)
        far1 = lax.ppermute(far1, "shard", back)
        tokens, far0 = lax.optimization_barrier((tokens, far0))
        own = pl.pallas_call(
            own_kernel,
            out_shape=jax.ShapeDtypeStruct((2, count, piece), BF16),
            in_specs=[hbm],
            out_specs=vmem,
            scratch_shapes=[pltpu.SemaphoreType.DMA((2,))],
            compiler_params=params,
            cost_estimate=pl.CostEstimate(flops=0, bytes_accessed=4 * count * piece, transcendentals=0),
        )(tokens)
        blocks = (own, ahead, far0, far1, behind)
    with jax.named_scope("momentum"):
        momentum, renewed = lax.optimization_barrier((momentum, renewed))
        new_momentum = pl.pallas_call(
            remain_kernel,
            out_shape=jax.ShapeDtypeStruct(momentum.shape, F32),
            in_specs=[hbm] * 4,
            out_specs=vmem,
            scratch_shapes=local_scratch + [pltpu.SemaphoreType.DMA((4,))],
            compiler_params=params,
            cost_estimate=pl.CostEstimate(flops=5 * 10**10, bytes_accessed=10**6, transcendentals=0),
        )(momentum, gradient, ordered_indices, table)
    with jax.named_scope("window"):
        window = lax.all_to_all(renewed, "shard", 0, 0).reshape(shards * rows, piece)
    with jax.named_scope("window_core"):
        window, *blocks = lax.optimization_barrier((window, *blocks))
        other = lax.ppermute(window, "replica", [(i, i ^ 1) for i in range(replicas)])
    with jax.named_scope("product"):
        size = shards * rows
        work = 2 * XS * count * size * piece
        first, rest = call(
            first_kernel,
            [
                jax.ShapeDtypeStruct((XS * count, size), F32),
                jax.ShapeDtypeStruct((XS * count, piece), BF16),
            ],
            *blocks,
            window,
            flops=work,
        )
        shape = (XS, count, size)
        ordered = call(second_kernel, jax.ShapeDtypeStruct(shape, BF16), rest, other, first, flops=work)
    with jax.named_scope("sum_x"):
        groups = [[y * XS + i for i in range(XS)] for y in range(YS)]
        parts = lax.all_to_all(ordered, "shard", 0, 0, axis_index_groups=groups)
        projected = call(finish_kernel, jax.ShapeDtypeStruct(shape[1:], BF16), parts)
    return projected, new_momentum


def solution(mesh):
    in_specs = (
        P(("shard", "replica"), None),
        P("shard", None),
        P("replica", "shard", None),
        P("replica", "shard", None),
        P("replica", "shard", None, None),
    )
    out_specs = (P(("shard", "replica"), None), P("replica", "shard", None))
    return jax.shard_map(local, mesh=mesh, in_specs=in_specs, out_specs=out_specs, check_vma=False)
```

```python
import numpy as np

import jax
import jax.numpy as jnp
from jax import lax
from jax.experimental import pallas as pl
from jax.experimental.pallas import tpu as pltpu
from jax.sharding import PartitionSpec as P

GROUP = 64
TOPK = 4
DECAY = 0.999
STEP = 0.01
PAIR = 2 * GROUP
XS = 4
YS = 8
MEMBERS = 2 * XS
VMEM_BYTES = 60 * 1024 * 1024
F32 = jnp.float32
BF16 = jnp.bfloat16
HIGH = lax.Precision.HIGHEST


def pair_table():
    k = np.arange(GROUP, dtype=np.float64)[:, None]
    n = np.arange(GROUP, dtype=np.float64)[None, :]
    c = np.cos(np.pi * (2.0 * n + 1.0) * k / (2.0 * GROUP)) * np.sqrt(2.0 / GROUP)
    c = c * np.where(k == 0, np.sqrt(0.5), 1.0)
    both = np.zeros((PAIR, PAIR), np.float64)
    both[:GROUP, :GROUP] = c
    both[GROUP:, GROUP:] = c
    return both.astype(np.float32)


def contract(a, b, da, db):
    return lax.dot_general(a, b, (((da,), (db,)), ((), ())), precision=HIGH, preferred_element_type=F32)


def forward_kernel(ahead, behind, far0, far1):
    far0[0] = ahead[2]
    far1[0] = behind[2]


def own_kernel(tokens, own, sems):
    x = lax.axis_index("shard") % XS
    piece = own.shape[2]
    halves = [pl.multiple_of((h * XS + x) * piece, 128) for h in range(2)]
    for copy in fetch([(tokens.at[:, pl.ds(at, piece)], own.at[h]) for h, at in enumerate(halves)], sems):
        copy.wait()


def lay_out(indices, lanes):
    rows, _, groups = indices.shape
    spread = lax.broadcasted_iota(jnp.int32, (rows, lanes), 1) % rows
    spread = jnp.where(spread == lax.broadcasted_iota(jnp.int32, (rows, lanes), 0), 1.0, 0.0).astype(BF16)
    pair = lax.broadcasted_iota(jnp.int32, (groups, lanes), 1) // rows
    transform = lax.broadcasted_iota(jnp.int32, (groups, lanes), 0)
    spreads = [
        lax.dot_general(
            indices[:, j, :].astype(F32).astype(BF16), spread, (((0,), (0,)), ((), ())), preferred_element_type=F32
        )
        for j in range(TOPK)
    ]
    return [
        jnp.sum(jnp.where(transform == 2 * pair + side, spreads[j], 0.0), axis=0, keepdims=True)
        for side in range(2)
        for j in range(TOPK)
    ]


def choose(momentum, gradient, index, table):
    rows, width = momentum.shape
    pairs = width // PAIR
    lanes = pairs * rows
    blended = DECAY * momentum + gradient.astype(F32)
    stacked = jnp.concatenate([blended[:, p * PAIR : (p + 1) * PAIR] for p in range(pairs)], axis=0)
    spectra = contract(table, stacked, 1, 1)
    freq = lax.broadcasted_iota(jnp.int32, (GROUP, lanes), 0).astype(F32)
    picked = []
    for side in range(2):
        part = spectra[side * GROUP : (side + 1) * GROUP]
        picked += [jnp.where(freq == index[side * TOPK + j], part, 0.0) for j in range(TOPK)]
    return blended, picked


def fetch(pairs, sems):
    copies = [pltpu.make_async_copy(a, b, sems.at[i]) for i, (a, b) in enumerate(pairs)]
    for copy in copies:
        copy.start()
    return copies


def send_kernel(momentum, gradient, indices, table, send, mom, grad, ind, tab, sems):
    first, *loads = fetch([(indices, ind), (momentum, mom), (gradient, grad), (table, tab)], sems)
    first.wait()
    index = lay_out(ind, mom.shape[1] * mom.shape[2] // PAIR)
    for load in loads:
        load.wait()
    _, picked = choose(mom[0], grad[0], index, tab[...])
    values = [jnp.sum(p, axis=0, keepdims=True) for p in picked]
    message = jnp.concatenate(values + index, axis=0).astype(BF16)
    half = message.shape[1] // 2
    for r in range(send.shape[0]):
        send[r] = message[:, r % 2 * half : (r % 2 + 1) * half]


def cut_kernel(tokens, ahead, behind, cut, sems):
    x = lax.axis_index("shard") % XS
    piece = cut.shape[2]
    pieces = []
    for i, (d, h) in enumerate([(1, 0), (1, 1), (2, 0), (3, 0), (3, 1), (2, 1)]):
        at = pl.multiple_of((h * XS + (x + d) % XS) * piece, 128)
        pieces.append((tokens.at[:, pl.ds(at, piece)], cut.at[i]))
    cuts = fetch(pieces, sems)
    outs = []
    for i, (first, number, out) in enumerate([(0, 3, ahead), (3, 3, behind)]):
        for c in cuts[first : first + number]:
            c.wait()
        outs += fetch([(cut.at[pl.ds(first, number)], out)], sems.at[pl.ds(len(pieces) + i, 1)])
    for out in outs:
        out.wait()


def remain_kernel(momentum, gradient, indices, table, new_momentum, mom, grad, ind, tab, sems):
    for load in fetch([(momentum, mom), (gradient, grad), (indices, ind), (table, tab)], sems):
        load.wait()
    rows = mom.shape[1]
    index = lay_out(ind, rows * mom.shape[2] // PAIR)
    blended, picked = choose(mom[0], grad[0], index, tab[...])
    kept = [sum(picked[side * TOPK + 1 : (side + 1) * TOPK], picked[side * TOPK]) for side in range(2)]
    field = contract(jnp.concatenate(kept, axis=0), tab[...], 0, 0)
    for p in range(blended.shape[1] // PAIR):
        at = slice(p * PAIR, (p + 1) * PAIR)
        new_momentum[0, :, at] = blended[:, at] - field[p * rows : (p + 1) * rows]


def renew_kernel(received, weight, table, renewed):
    replicas, _, lanes = received.shape
    rows = weight.shape[0]
    half = weight.shape[1] // 2
    core = lax.axis_index("replica") % 2
    freq = lax.broadcasted_iota(jnp.int32, (GROUP, 128), 0).astype(F32).astype(BF16)
    columns = []
    for c in range(lanes // 128):
        at = slice(c * 128, (c + 1) * 128)
        sums = [jnp.zeros((GROUP, 128), F32) for _ in range(2)]
        for r in range(replicas):
            message = received[r, :, at]
            for side in range(2):
                dense = jnp.zeros((GROUP, 128), BF16)
                for row in range(side * TOPK, (side + 1) * TOPK):
                    dense = jnp.where(freq == message[2 * TOPK + row][None, :], message[row][None, :], dense)
                sums[side] = sums[side] + dense.astype(F32)
        columns.append(jnp.concatenate(sums, axis=0))
    field = contract(jnp.concatenate(columns, axis=1), table[...], 0, 0)
    old = weight[:, pl.ds(pl.multiple_of(core * half, 128), half)].astype(F32)
    per = half // XS // PAIR
    for x in range(XS):
        for p in range(per):
            q = x * per + p
            new = old[:, q * PAIR : (q + 1) * PAIR] - STEP * field[q * rows : (q + 1) * rows]
            new = new.astype(BF16)
            for y in range(YS):
                renewed[y * XS + x, :, p * PAIR : (p + 1) * PAIR] = new


def stack(own, ahead, far0, far1, behind, h):
    return jnp.concatenate([own[h], ahead[h], jnp.where(h == 0, far0[0], far1[0]), behind[h]], axis=0)


def product(tokens, window):
    return lax.dot_general(tokens, window[...], (((1,), (1,)), ((), ())), preferred_element_type=F32)


def first_kernel(*refs):
    *blocks, window, out, rest = refs
    core = lax.axis_index("replica") % 2
    out[...] = product(stack(*blocks, core), window)
    rest[...] = stack(*blocks, 1 - core)


def second_kernel(rest, window, first, out, ready, sems):
    x = lax.axis_index("shard") % XS
    count = ready.shape[1]
    copies = []
    for i in range(0, XS, 2):
        at = slice(i * count, (i + 2) * count)
        total = first[at] + product(rest[at], window)
        for d in range(i, i + 2):
            ready[d] = total[(d - i) * count : (d - i + 1) * count].astype(BF16)
            copies += fetch([(ready.at[d], out.at[(x + XS - d) % XS])], sems.at[pl.ds(d, 1)])
    for copy in copies:
        copy.wait()


def finish_kernel(parts, out):
    total = parts[0].astype(F32)
    for x in range(1, XS):
        total = total + parts[x].astype(F32)
    out[...] = total.astype(BF16)


def call(kernel, out, *args, flops=0, space=pltpu.VMEM, scratch=()):
    out_list = jax.tree.leaves(out)
    moved = sum(a.size * a.dtype.itemsize for a in args) + sum(o.size * o.dtype.itemsize for o in out_list)
    return pl.pallas_call(
        kernel,
        out_shape=out,
        in_specs=[pl.BlockSpec(memory_space=pltpu.VMEM)] * len(args),
        out_specs=jax.tree.map(lambda _: pl.BlockSpec(memory_space=space), out),
        scratch_shapes=list(scratch),
        compiler_params=pltpu.CompilerParams(vmem_limit_bytes=20 * 1024 * 1024),
        cost_estimate=pl.CostEstimate(flops=flops, bytes_accessed=moved, transcendentals=0),
    )(*args)


def local(tokens, weight, momentum, gradient, indices):
    count, width = tokens.shape
    rows = weight.shape[0]
    half, piece = width // 2, width // 2 // XS
    table = jnp.asarray(pair_table())
    replicas = lax.axis_size("replica")
    shards = lax.axis_size("shard")

    lanes = width // PAIR * rows
    ordered_indices = indices[0].transpose(0, 2, 1)
    local_scratch = [
        pltpu.VMEM(momentum.shape, F32),
        pltpu.VMEM(gradient.shape, BF16),
        pltpu.VMEM(ordered_indices.shape, jnp.int32),
        pltpu.VMEM(table.shape, F32),
    ]
    hbm, vmem = pl.BlockSpec(memory_space=pltpu.HBM), pl.BlockSpec(memory_space=pltpu.VMEM)
    params = pltpu.CompilerParams(vmem_limit_bytes=VMEM_BYTES)
    with jax.named_scope("coefficients"):
        send = pl.pallas_call(
            send_kernel,
            out_shape=jax.ShapeDtypeStruct((replicas, 4 * TOPK, lanes // 2), BF16),
            in_specs=[hbm] * 4,
            out_specs=vmem,
            scratch_shapes=local_scratch + [pltpu.SemaphoreType.DMA((4,))],
            compiler_params=params,
            cost_estimate=pl.CostEstimate(flops=10**8, bytes_accessed=10**6, transcendentals=0),
        )(momentum, gradient, ordered_indices, table)
    with jax.named_scope("cut"):
        tokens, send = lax.optimization_barrier((tokens, send))
        ahead, behind = pl.pallas_call(
            cut_kernel,
            out_shape=[jax.ShapeDtypeStruct((n, count, piece), BF16) for n in (3, 3)],
            in_specs=[hbm],
            out_specs=[hbm] * 2,
            scratch_shapes=[pltpu.VMEM((6, count, piece), BF16), pltpu.SemaphoreType.DMA((8,))],
            compiler_params=params,
            cost_estimate=pl.CostEstimate(flops=0, bytes_accessed=4 * tokens.size, transcendentals=0),
        )(tokens)

    with jax.named_scope("exchange"):
        received = lax.all_to_all(send, "replica", 0, 0)
    with jax.named_scope("renew"):
        renewed = call(
            renew_kernel,
            jax.ShapeDtypeStruct((shards, rows, piece), BF16),
            received,
            weight,
            table,
            flops=10**10,
        )
    with jax.named_scope("tokens_x"):
        on, back = (
            [(s, s // XS * XS + (s + step) % XS) for s in range(shards)] for step in (1, XS - 1)
        )
        ahead = lax.ppermute(ahead, "shard", on)
        behind = lax.ppermute(behind, "shard", back)
        one = jax.ShapeDtypeStruct((1, count, piece), BF16)
        far0, far1 = call(forward_kernel, [one, one], ahead, behind, flops=5 * 10**10)
        far0 = lax.ppermute(far0, "shard", on)
        far1 = lax.ppermute(far1, "shard", back)
        tokens, far0 = lax.optimization_barrier((tokens, far0))
        own = pl.pallas_call(
            own_kernel,
            out_shape=jax.ShapeDtypeStruct((2, count, piece), BF16),
            in_specs=[hbm],
            out_specs=vmem,
            scratch_shapes=[pltpu.SemaphoreType.DMA((2,))],
            compiler_params=pltpu.CompilerParams(vmem_limit_bytes=20 * 1024 * 1024),
            cost_estimate=pl.CostEstimate(flops=0, bytes_accessed=4 * count * piece, transcendentals=0),
        )(tokens)
        blocks = (own, ahead, far0, far1, behind)
    with jax.named_scope("momentum"):
        momentum, renewed = lax.optimization_barrier((momentum, renewed))
        new_momentum = pl.pallas_call(
            remain_kernel,
            out_shape=jax.ShapeDtypeStruct(momentum.shape, F32),
            in_specs=[hbm] * 4,
            out_specs=vmem,
            scratch_shapes=local_scratch + [pltpu.SemaphoreType.DMA((4,))],
            compiler_params=params,
            cost_estimate=pl.CostEstimate(flops=5 * 10**10, bytes_accessed=10**6, transcendentals=0),
        )(momentum, gradient, ordered_indices, table)
    with jax.named_scope("window"):
        window = lax.all_to_all(renewed, "shard", 0, 0).reshape(shards * rows, piece)
    with jax.named_scope("window_core"):
        window, *blocks = lax.optimization_barrier((window, *blocks))
        other = lax.ppermute(window, "replica", [(i, i ^ 1) for i in range(replicas)])
    with jax.named_scope("product"):
        size = shards * rows
        work = 2 * XS * count * size * piece
        first, rest = call(
            first_kernel,
            [
                jax.ShapeDtypeStruct((XS * count, size), F32),
                jax.ShapeDtypeStruct((XS * count, piece), BF16),
            ],
            *blocks,
            window,
            flops=work,
        )
        shape = (XS, count, size)
        ordered = call(
            second_kernel,
            jax.ShapeDtypeStruct(shape, BF16),
            rest,
            other,
            first,
            flops=work,
            space=pltpu.HBM,
            scratch=(pltpu.VMEM(shape, BF16), pltpu.SemaphoreType.DMA((XS,))),
        )
    with jax.named_scope("sum_x"):
        groups = [[y * XS + i for i in range(XS)] for y in range(YS)]
        parts = lax.all_to_all(ordered, "shard", 0, 0, axis_index_groups=groups)
        projected = call(finish_kernel, jax.ShapeDtypeStruct(shape[1:], BF16), parts)
    return projected, new_momentum


def solution(mesh):
    in_specs = (
        P(("shard", "replica"), None),
        P("shard", None),
        P("replica", "shard", None),
        P("replica", "shard", None),
        P("replica", "shard", None, None),
    )
    out_specs = (P(("shard", "replica"), None), P("replica", "shard", None))
    return jax.shard_map(local, mesh=mesh, in_specs=in_specs, out_specs=out_specs, check_vma=False)
```

```python
import numpy as np

import jax
import jax.numpy as jnp
from jax import lax
from jax.experimental import pallas as pl
from jax.experimental.pallas import tpu as pltpu
from jax.sharding import PartitionSpec as P

GROUP = 64
TOPK = 4
DECAY = 0.999
STEP = 0.01
PAIR = 2 * GROUP
XS = 4
YS = 8
MEMBERS = 2 * XS
VMEM_BYTES = 60 * 1024 * 1024
F32 = jnp.float32
BF16 = jnp.bfloat16
HIGH = lax.Precision.HIGHEST


def pair_table():
    k = np.arange(GROUP, dtype=np.float64)[:, None]
    n = np.arange(GROUP, dtype=np.float64)[None, :]
    c = np.cos(np.pi * (2.0 * n + 1.0) * k / (2.0 * GROUP)) * np.sqrt(2.0 / GROUP)
    c = c * np.where(k == 0, np.sqrt(0.5), 1.0)
    both = np.zeros((PAIR, PAIR), np.float64)
    both[:GROUP, :GROUP] = c
    both[GROUP:, GROUP:] = c
    return both.astype(np.float32)


def contract(a, b, da, db):
    return lax.dot_general(a, b, (((da,), (db,)), ((), ())), precision=HIGH, preferred_element_type=F32)


def forward_kernel(ahead, behind, far0, far1):
    far0[0] = ahead[2]
    far1[0] = behind[2]


def own_kernel(tokens, own, sems):
    x = lax.axis_index("shard") % XS
    piece = own.shape[2]
    halves = [pl.multiple_of((h * XS + x) * piece, 128) for h in range(2)]
    for copy in fetch([(tokens.at[:, pl.ds(at, piece)], own.at[h]) for h, at in enumerate(halves)], sems):
        copy.wait()


def lay_out(indices, lanes):
    rows, _, groups = indices.shape
    spread = lax.broadcasted_iota(jnp.int32, (rows, lanes), 1) % rows
    spread = jnp.where(spread == lax.broadcasted_iota(jnp.int32, (rows, lanes), 0), 1.0, 0.0).astype(BF16)
    pair = lax.broadcasted_iota(jnp.int32, (groups, lanes), 1) // rows
    transform = lax.broadcasted_iota(jnp.int32, (groups, lanes), 0)
    spreads = [
        lax.dot_general(
            indices[:, j, :].astype(F32).astype(BF16), spread, (((0,), (0,)), ((), ())), preferred_element_type=F32
        )
        for j in range(TOPK)
    ]
    return [
        jnp.sum(jnp.where(transform == 2 * pair + side, spreads[j], 0.0), axis=0, keepdims=True)
        for side in range(2)
        for j in range(TOPK)
    ]


def choose(momentum, gradient, index, table):
    rows, width = momentum.shape
    pairs = width // PAIR
    lanes = pairs * rows
    blended = DECAY * momentum + gradient.astype(F32)
    stacked = jnp.concatenate([blended[:, p * PAIR : (p + 1) * PAIR] for p in range(pairs)], axis=0)
    spectra = contract(table, stacked, 1, 1)
    freq = lax.broadcasted_iota(jnp.int32, (GROUP, lanes), 0).astype(F32)
    picked = []
    for side in range(2):
        part = spectra[side * GROUP : (side + 1) * GROUP]
        picked += [jnp.where(freq == index[side * TOPK + j], part, 0.0) for j in range(TOPK)]
    return blended, picked


def fetch(pairs, sems):
    copies = [pltpu.make_async_copy(a, b, sems.at[i]) for i, (a, b) in enumerate(pairs)]
    for copy in copies:
        copy.start()
    return copies


def send_kernel(momentum, gradient, indices, table, send, mom, grad, ind, tab, sems):
    first, *loads = fetch([(indices, ind), (momentum, mom), (gradient, grad), (table, tab)], sems)
    first.wait()
    index = lay_out(ind, mom.shape[1] * mom.shape[2] // PAIR)
    for load in loads:
        load.wait()
    _, picked = choose(mom[0], grad[0], index, tab[...])
    values = [jnp.sum(p, axis=0, keepdims=True) for p in picked]
    message = jnp.concatenate(values + index, axis=0).astype(BF16)
    half = message.shape[1] // 2
    for r in range(send.shape[0]):
        send[r] = message[:, r % 2 * half : (r % 2 + 1) * half]


def cut_kernel(tokens, ahead, behind, cut, sems):
    x = lax.axis_index("shard") % XS
    piece = cut.shape[2]
    pieces = []
    for i, (d, h) in enumerate([(1, 0), (1, 1), (2, 0), (3, 0), (3, 1), (2, 1)]):
        at = pl.multiple_of((h * XS + (x + d) % XS) * piece, 128)
        pieces.append((tokens.at[:, pl.ds(at, piece)], cut.at[i]))
    cuts = fetch(pieces, sems)
    outs = []
    for i, (first, number, out) in enumerate([(0, 3, ahead), (3, 3, behind)]):
        for c in cuts[first : first + number]:
            c.wait()
        outs += fetch([(cut.at[pl.ds(first, number)], out)], sems.at[pl.ds(len(pieces) + i, 1)])
    for out in outs:
        out.wait()


def remain_kernel(momentum, gradient, indices, table, new_momentum, mom, grad, ind, tab, sems):
    for load in fetch([(momentum, mom), (gradient, grad), (indices, ind), (table, tab)], sems):
        load.wait()
    rows = mom.shape[1]
    index = lay_out(ind, rows * mom.shape[2] // PAIR)
    blended, picked = choose(mom[0], grad[0], index, tab[...])
    kept = [sum(picked[side * TOPK + 1 : (side + 1) * TOPK], picked[side * TOPK]) for side in range(2)]
    field = contract(jnp.concatenate(kept, axis=0), tab[...], 0, 0)
    for p in range(blended.shape[1] // PAIR):
        at = slice(p * PAIR, (p + 1) * PAIR)
        new_momentum[0, :, at] = blended[:, at] - field[p * rows : (p + 1) * rows]


def renew_kernel(received, weight, table, renewed):
    replicas, _, lanes = received.shape
    rows = weight.shape[0]
    half = weight.shape[1] // 2
    core = lax.axis_index("replica") % 2
    freq = lax.broadcasted_iota(jnp.int32, (GROUP, 128), 0).astype(F32).astype(BF16)
    columns = []
    for c in range(lanes // 128):
        at = slice(c * 128, (c + 1) * 128)
        sums = [jnp.zeros((GROUP, 128), F32) for _ in range(2)]
        for r in range(replicas):
            message = received[r, :, at]
            for side in range(2):
                dense = jnp.zeros((GROUP, 128), BF16)
                for row in range(side * TOPK, (side + 1) * TOPK):
                    dense = jnp.where(freq == message[2 * TOPK + row][None, :], message[row][None, :], dense)
                sums[side] = sums[side] + dense.astype(F32)
        columns.append(jnp.concatenate(sums, axis=0))
    field = contract(jnp.concatenate(columns, axis=1), table[...], 0, 0)
    old = weight[:, pl.ds(pl.multiple_of(core * half, 128), half)].astype(F32)
    per = half // XS // PAIR
    for x in range(XS):
        for p in range(per):
            q = x * per + p
            new = old[:, q * PAIR : (q + 1) * PAIR] - STEP * field[q * rows : (q + 1) * rows]
            new = new.astype(BF16)
            for y in range(YS):
                renewed[y * XS + x, :, p * PAIR : (p + 1) * PAIR] = new


def stack(own, ahead, far0, far1, behind, h):
    return jnp.concatenate([own[h], ahead[h], jnp.where(h == 0, far0[0], far1[0]), behind[h]], axis=0)


def product(tokens, window):
    return lax.dot_general(tokens, window[...], (((1,), (1,)), ((), ())), preferred_element_type=F32)


def first_kernel(*refs):
    *blocks, window, out, rest = refs
    core = lax.axis_index("replica") % 2
    out[...] = product(stack(*blocks, core), window)
    rest[...] = stack(*blocks, 1 - core)


def second_kernel(rest, window, first, out):
    x = lax.axis_index("shard") % XS
    count = out.shape[1]
    total = first[...] + product(rest[...], window)
    for d in range(XS):
        out[(x + XS - d) % XS] = total[d * count : (d + 1) * count].astype(BF16)


def finish_kernel(parts, out):
    total = parts[0].astype(F32)
    for x in range(1, XS):
        total = total + parts[x].astype(F32)
    out[...] = total.astype(BF16)


def call(kernel, out, *args, flops=0):
    out_list = jax.tree.leaves(out)
    moved = sum(a.size * a.dtype.itemsize for a in args) + sum(o.size * o.dtype.itemsize for o in out_list)
    return pl.pallas_call(
        kernel,
        out_shape=out,
        in_specs=[pl.BlockSpec(memory_space=pltpu.VMEM)] * len(args),
        out_specs=jax.tree.map(lambda _: pl.BlockSpec(memory_space=pltpu.VMEM), out),
        compiler_params=pltpu.CompilerParams(vmem_limit_bytes=20 * 1024 * 1024),
        cost_estimate=pl.CostEstimate(flops=flops, bytes_accessed=moved, transcendentals=0),
    )(*args)


def local(tokens, weight, momentum, gradient, indices):
    count, width = tokens.shape
    rows = weight.shape[0]
    half, piece = width // 2, width // 2 // XS
    table = jnp.asarray(pair_table())
    replicas = lax.axis_size("replica")
    shards = lax.axis_size("shard")

    lanes = width // PAIR * rows
    ordered_indices = indices[0].transpose(0, 2, 1)
    local_scratch = [
        pltpu.VMEM(momentum.shape, F32),
        pltpu.VMEM(gradient.shape, BF16),
        pltpu.VMEM(ordered_indices.shape, jnp.int32),
        pltpu.VMEM(table.shape, F32),
    ]
    hbm, vmem = pl.BlockSpec(memory_space=pltpu.HBM), pl.BlockSpec(memory_space=pltpu.VMEM)
    params = pltpu.CompilerParams(vmem_limit_bytes=VMEM_BYTES)
    with jax.named_scope("coefficients"):
        send = pl.pallas_call(
            send_kernel,
            out_shape=jax.ShapeDtypeStruct((replicas, 4 * TOPK, lanes // 2), BF16),
            in_specs=[hbm] * 4,
            out_specs=vmem,
            scratch_shapes=local_scratch + [pltpu.SemaphoreType.DMA((4,))],
            compiler_params=params,
            cost_estimate=pl.CostEstimate(flops=10**8, bytes_accessed=10**6, transcendentals=0),
        )(momentum, gradient, ordered_indices, table)
    with jax.named_scope("cut"):
        tokens, send = lax.optimization_barrier((tokens, send))
        ahead, behind = pl.pallas_call(
            cut_kernel,
            out_shape=[jax.ShapeDtypeStruct((n, count, piece), BF16) for n in (3, 3)],
            in_specs=[hbm],
            out_specs=[hbm] * 2,
            scratch_shapes=[pltpu.VMEM((6, count, piece), BF16), pltpu.SemaphoreType.DMA((8,))],
            compiler_params=params,
            cost_estimate=pl.CostEstimate(flops=0, bytes_accessed=4 * tokens.size, transcendentals=0),
        )(tokens)

    with jax.named_scope("exchange"):
        received = lax.all_to_all(send, "replica", 0, 0)
    with jax.named_scope("renew"):
        renewed = call(
            renew_kernel,
            jax.ShapeDtypeStruct((shards, rows, piece), BF16),
            received,
            weight,
            table,
            flops=10**10,
        )
    with jax.named_scope("tokens_x"):
        on, back = (
            [(s, s // XS * XS + (s + step) % XS) for s in range(shards)] for step in (1, XS - 1)
        )
        ahead = lax.ppermute(ahead, "shard", on)
        behind = lax.ppermute(behind, "shard", back)
        one = jax.ShapeDtypeStruct((1, count, piece), BF16)
        far0, far1 = call(forward_kernel, [one, one], ahead, behind, flops=5 * 10**10)
        momentum, _ = lax.optimization_barrier((momentum, far0))
        far0 = lax.ppermute(far0, "shard", on)
        far1 = lax.ppermute(far1, "shard", back)
        tokens, far0 = lax.optimization_barrier((tokens, far0))
        own = pl.pallas_call(
            own_kernel,
            out_shape=jax.ShapeDtypeStruct((2, count, piece), BF16),
            in_specs=[hbm],
            out_specs=vmem,
            scratch_shapes=[pltpu.SemaphoreType.DMA((2,))],
            compiler_params=pltpu.CompilerParams(vmem_limit_bytes=20 * 1024 * 1024),
            cost_estimate=pl.CostEstimate(flops=0, bytes_accessed=4 * count * piece, transcendentals=0),
        )(tokens)
        blocks = (own, ahead, far0, far1, behind)
    with jax.named_scope("momentum"):
        new_momentum = pl.pallas_call(
            remain_kernel,
            out_shape=jax.ShapeDtypeStruct(momentum.shape, F32),
            in_specs=[hbm] * 4,
            out_specs=vmem,
            scratch_shapes=local_scratch + [pltpu.SemaphoreType.DMA((4,))],
            compiler_params=params,
            cost_estimate=pl.CostEstimate(flops=10**9, bytes_accessed=10**6, transcendentals=0),
        )(momentum, gradient, ordered_indices, table)
    with jax.named_scope("window"):
        window = lax.all_to_all(renewed, "shard", 0, 0).reshape(shards * rows, piece)
    with jax.named_scope("window_core"):
        window, new_momentum, *blocks = lax.optimization_barrier((window, new_momentum, *blocks))
        other = lax.ppermute(window, "replica", [(i, i ^ 1) for i in range(replicas)])
    with jax.named_scope("product"):
        size = shards * rows
        work = 2 * XS * count * size * piece
        first, rest = call(
            first_kernel,
            [
                jax.ShapeDtypeStruct((XS * count, size), F32),
                jax.ShapeDtypeStruct((XS * count, piece), BF16),
            ],
            *blocks,
            window,
            flops=work,
        )
        shape = (XS, count, size)
        ordered = call(
            second_kernel,
            jax.ShapeDtypeStruct(shape, BF16),
            rest,
            other,
            first,
            flops=work,
        )
    with jax.named_scope("sum_x"):
        groups = [[y * XS + i for i in range(XS)] for y in range(YS)]
        parts = lax.all_to_all(ordered, "shard", 0, 0, axis_index_groups=groups)
        projected = call(finish_kernel, jax.ShapeDtypeStruct(shape[1:], BF16), parts)
    return projected, new_momentum


def solution(mesh):
    in_specs = (
        P(("shard", "replica"), None),
        P("shard", None),
        P("replica", "shard", None),
        P("replica", "shard", None),
        P("replica", "shard", None, None),
    )
    out_specs = (P(("shard", "replica"), None), P("replica", "shard", None))
    return jax.shard_map(local, mesh=mesh, in_specs=in_specs, out_specs=out_specs, check_vma=False)
```

```python
import numpy as np

import jax
import jax.numpy as jnp
from jax import lax
from jax.experimental import pallas as pl
from jax.experimental.pallas import tpu as pltpu
from jax.sharding import PartitionSpec as P

GROUP = 64
TOPK = 4
DECAY = 0.999
STEP = 0.01
PAIR = 2 * GROUP
XS = 4
YS = 8
MEMBERS = 2 * XS
VMEM_BYTES = 60 * 1024 * 1024
F32 = jnp.float32
BF16 = jnp.bfloat16
HIGH = lax.Precision.HIGHEST


def pair_table():
    k = np.arange(GROUP, dtype=np.float64)[:, None]
    n = np.arange(GROUP, dtype=np.float64)[None, :]
    c = np.cos(np.pi * (2.0 * n + 1.0) * k / (2.0 * GROUP)) * np.sqrt(2.0 / GROUP)
    c = c * np.where(k == 0, np.sqrt(0.5), 1.0)
    both = np.zeros((PAIR, PAIR), np.float64)
    both[:GROUP, :GROUP] = c
    both[GROUP:, GROUP:] = c
    return both.astype(np.float32)


def contract(a, b, da, db):
    return lax.dot_general(a, b, (((da,), (db,)), ((), ())), precision=HIGH, preferred_element_type=F32)


def forward_kernel(ahead, behind, far0, far1):
    far0[0] = ahead[2]
    far1[0] = behind[2]


def own_kernel(tokens, own, sems):
    x = lax.axis_index("shard") % XS
    piece = own.shape[2]
    halves = [pl.multiple_of((h * XS + x) * piece, 128) for h in range(2)]
    for copy in fetch([(tokens.at[:, pl.ds(at, piece)], own.at[h]) for h, at in enumerate(halves)], sems):
        copy.wait()


def lay_out(indices, lanes):
    rows, _, groups = indices.shape
    spread = lax.broadcasted_iota(jnp.int32, (rows, lanes), 1) % rows
    spread = jnp.where(spread == lax.broadcasted_iota(jnp.int32, (rows, lanes), 0), 1.0, 0.0).astype(BF16)
    pair = lax.broadcasted_iota(jnp.int32, (groups, lanes), 1) // rows
    transform = lax.broadcasted_iota(jnp.int32, (groups, lanes), 0)
    spreads = [
        lax.dot_general(
            indices[:, j, :].astype(F32).astype(BF16), spread, (((0,), (0,)), ((), ())), preferred_element_type=F32
        )
        for j in range(TOPK)
    ]
    return [
        jnp.sum(jnp.where(transform == 2 * pair + side, spreads[j], 0.0), axis=0, keepdims=True)
        for side in range(2)
        for j in range(TOPK)
    ]


def choose(momentum, gradient, index, table):
    rows, width = momentum.shape
    pairs = width // PAIR
    lanes = pairs * rows
    blended = DECAY * momentum + gradient.astype(F32)
    stacked = jnp.concatenate([blended[:, p * PAIR : (p + 1) * PAIR] for p in range(pairs)], axis=0)
    spectra = contract(table, stacked, 1, 1)
    freq = lax.broadcasted_iota(jnp.int32, (GROUP, lanes), 0).astype(F32)
    picked = []
    for side in range(2):
        part = spectra[side * GROUP : (side + 1) * GROUP]
        picked += [jnp.where(freq == index[side * TOPK + j], part, 0.0) for j in range(TOPK)]
    return blended, picked


def fetch(pairs, sems):
    copies = [pltpu.make_async_copy(a, b, sems.at[i]) for i, (a, b) in enumerate(pairs)]
    for copy in copies:
        copy.start()
    return copies


def send_kernel(momentum, gradient, indices, table, send, mom, grad, ind, tab, sems):
    first, *loads = fetch([(indices, ind), (momentum, mom), (gradient, grad), (table, tab)], sems)
    first.wait()
    index = lay_out(ind, mom.shape[1] * mom.shape[2] // PAIR)
    for load in loads:
        load.wait()
    _, picked = choose(mom[0], grad[0], index, tab[...])
    values = [jnp.sum(p, axis=0, keepdims=True) for p in picked]
    message = jnp.concatenate(values + index, axis=0).astype(BF16)
    half = message.shape[1] // 2
    for r in range(send.shape[0]):
        send[r] = message[:, r % 2 * half : (r % 2 + 1) * half]


def cut_kernel(tokens, ahead, behind, cut, sems):
    x = lax.axis_index("shard") % XS
    piece = cut.shape[2]
    pieces = []
    for i, (d, h) in enumerate([(1, 0), (1, 1), (2, 0), (3, 0), (3, 1), (2, 1)]):
        at = pl.multiple_of((h * XS + (x + d) % XS) * piece, 128)
        pieces.append((tokens.at[:, pl.ds(at, piece)], cut.at[i]))
    cuts = fetch(pieces, sems)
    outs = []
    for i, (first, number, out) in enumerate([(0, 3, ahead), (3, 3, behind)]):
        for c in cuts[first : first + number]:
            c.wait()
        outs += fetch([(cut.at[pl.ds(first, number)], out)], sems.at[pl.ds(len(pieces) + i, 1)])
    for out in outs:
        out.wait()


def remain_kernel(momentum, gradient, indices, table, new_momentum, mom, grad, ind, tab, sems):
    for load in fetch([(momentum, mom), (gradient, grad), (indices, ind), (table, tab)], sems):
        load.wait()
    rows = mom.shape[1]
    index = lay_out(ind, rows * mom.shape[2] // PAIR)
    blended, picked = choose(mom[0], grad[0], index, tab[...])
    kept = [sum(picked[side * TOPK + 1 : (side + 1) * TOPK], picked[side * TOPK]) for side in range(2)]
    field = contract(jnp.concatenate(kept, axis=0), tab[...], 0, 0)
    for p in range(blended.shape[1] // PAIR):
        at = slice(p * PAIR, (p + 1) * PAIR)
        new_momentum[0, :, at] = blended[:, at] - field[p * rows : (p + 1) * rows]


def renew_kernel(received, weight, table, renewed):
    replicas, _, lanes = received.shape
    rows = weight.shape[0]
    half = weight.shape[1] // 2
    core = lax.axis_index("replica") % 2
    freq = lax.broadcasted_iota(jnp.int32, (GROUP, 128), 0).astype(F32).astype(BF16)
    columns = []
    for c in range(lanes // 128):
        at = slice(c * 128, (c + 1) * 128)
        sums = [jnp.zeros((GROUP, 128), F32) for _ in range(2)]
        for r in range(replicas):
            message = received[r, :, at]
            for side in range(2):
                dense = jnp.zeros((GROUP, 128), BF16)
                for row in range(side * TOPK, (side + 1) * TOPK):
                    dense = jnp.where(freq == message[2 * TOPK + row][None, :], message[row][None, :], dense)
                sums[side] = sums[side] + dense.astype(F32)
        columns.append(jnp.concatenate(sums, axis=0))
    field = contract(jnp.concatenate(columns, axis=1), table[...], 0, 0)
    old = weight[:, pl.ds(pl.multiple_of(core * half, 128), half)].astype(F32)
    per = half // XS // PAIR
    for x in range(XS):
        for p in range(per):
            q = x * per + p
            new = old[:, q * PAIR : (q + 1) * PAIR] - STEP * field[q * rows : (q + 1) * rows]
            new = new.astype(BF16)
            for y in range(YS):
                renewed[y * XS + x, :, p * PAIR : (p + 1) * PAIR] = new


def stack(own, ahead, far0, far1, behind, h):
    return jnp.concatenate([own[h], ahead[h], jnp.where(h == 0, far0[0], far1[0]), behind[h]], axis=0)


def product(tokens, window):
    return lax.dot_general(tokens, window[...], (((1,), (1,)), ((), ())), preferred_element_type=F32)


def first_kernel(*refs):
    *blocks, window, out, rest = refs
    core = lax.axis_index("replica") % 2
    out[...] = product(stack(*blocks, core), window)
    rest[...] = stack(*blocks, 1 - core)


def second_kernel(rest, window, first, out):
    x = lax.axis_index("shard") % XS
    count = out.shape[1]
    total = first[...] + product(rest[...], window)
    for d in range(XS):
        out[(x + XS - d) % XS] = total[d * count : (d + 1) * count].astype(BF16)


def finish_kernel(parts, out):
    total = parts[0].astype(F32)
    for x in range(1, XS):
        total = total + parts[x].astype(F32)
    out[...] = total.astype(BF16)


def call(kernel, out, *args, flops=0):
    out_list = jax.tree.leaves(out)
    moved = sum(a.size * a.dtype.itemsize for a in args) + sum(o.size * o.dtype.itemsize for o in out_list)
    return pl.pallas_call(
        kernel,
        out_shape=out,
        in_specs=[pl.BlockSpec(memory_space=pltpu.VMEM)] * len(args),
        out_specs=jax.tree.map(lambda _: pl.BlockSpec(memory_space=pltpu.VMEM), out),
        compiler_params=pltpu.CompilerParams(vmem_limit_bytes=20 * 1024 * 1024),
        cost_estimate=pl.CostEstimate(flops=flops, bytes_accessed=moved, transcendentals=0),
    )(*args)


def local(tokens, weight, momentum, gradient, indices):
    count, width = tokens.shape
    rows = weight.shape[0]
    half, piece = width // 2, width // 2 // XS
    table = jnp.asarray(pair_table())
    replicas = lax.axis_size("replica")
    shards = lax.axis_size("shard")

    lanes = width // PAIR * rows
    ordered_indices = indices[0].transpose(0, 2, 1)
    local_scratch = [
        pltpu.VMEM(momentum.shape, F32),
        pltpu.VMEM(gradient.shape, BF16),
        pltpu.VMEM(ordered_indices.shape, jnp.int32),
        pltpu.VMEM(table.shape, F32),
    ]
    hbm, vmem = pl.BlockSpec(memory_space=pltpu.HBM), pl.BlockSpec(memory_space=pltpu.VMEM)
    params = pltpu.CompilerParams(vmem_limit_bytes=VMEM_BYTES)
    with jax.named_scope("coefficients"):
        send = pl.pallas_call(
            send_kernel,
            out_shape=jax.ShapeDtypeStruct((replicas, 4 * TOPK, lanes // 2), BF16),
            in_specs=[hbm] * 4,
            out_specs=vmem,
            scratch_shapes=local_scratch + [pltpu.SemaphoreType.DMA((4,))],
            compiler_params=params,
            cost_estimate=pl.CostEstimate(flops=10**8, bytes_accessed=10**6, transcendentals=0),
        )(momentum, gradient, ordered_indices, table)
    with jax.named_scope("cut"):
        tokens, send = lax.optimization_barrier((tokens, send))
        ahead, behind = pl.pallas_call(
            cut_kernel,
            out_shape=[jax.ShapeDtypeStruct((n, count, piece), BF16) for n in (3, 3)],
            in_specs=[hbm],
            out_specs=[hbm] * 2,
            scratch_shapes=[pltpu.VMEM((6, count, piece), BF16), pltpu.SemaphoreType.DMA((8,))],
            compiler_params=params,
            cost_estimate=pl.CostEstimate(flops=0, bytes_accessed=4 * tokens.size, transcendentals=0),
        )(tokens)

    with jax.named_scope("exchange"):
        received = lax.all_to_all(send, "replica", 0, 0)
    with jax.named_scope("renew"):
        renewed = call(
            renew_kernel,
            jax.ShapeDtypeStruct((shards, rows, piece), BF16),
            received,
            weight,
            table,
            flops=10**10,
        )
    with jax.named_scope("tokens_x"):
        on, back = (
            [(s, s // XS * XS + (s + step) % XS) for s in range(shards)] for step in (1, XS - 1)
        )
        ahead = lax.ppermute(ahead, "shard", on)
        behind = lax.ppermute(behind, "shard", back)
        one = jax.ShapeDtypeStruct((1, count, piece), BF16)
        far0, far1 = call(forward_kernel, [one, one], ahead, behind, flops=5 * 10**10)
        momentum, _ = lax.optimization_barrier((momentum, far0))
        far0 = lax.ppermute(far0, "shard", on)
        far1 = lax.ppermute(far1, "shard", back)
        tokens, far0 = lax.optimization_barrier((tokens, far0))
        own = pl.pallas_call(
            own_kernel,
            out_shape=jax.ShapeDtypeStruct((2, count, piece), BF16),
            in_specs=[hbm],
            out_specs=vmem,
            scratch_shapes=[pltpu.SemaphoreType.DMA((2,))],
            compiler_params=pltpu.CompilerParams(vmem_limit_bytes=20 * 1024 * 1024),
            cost_estimate=pl.CostEstimate(flops=0, bytes_accessed=4 * count * piece, transcendentals=0),
        )(tokens)
        blocks = (own, ahead, far0, far1, behind)
    with jax.named_scope("momentum"):
        new_momentum = pl.pallas_call(
            remain_kernel,
            out_shape=jax.ShapeDtypeStruct(momentum.shape, F32),
            in_specs=[hbm] * 4,
            out_specs=vmem,
            scratch_shapes=local_scratch + [pltpu.SemaphoreType.DMA((4,))],
            compiler_params=pltpu.CompilerParams(vmem_limit_bytes=40 * 1024 * 1024),
            cost_estimate=pl.CostEstimate(flops=10**9, bytes_accessed=10**6, transcendentals=0),
        )(momentum, gradient, ordered_indices, table)
    with jax.named_scope("window"):
        window = lax.all_to_all(renewed, "shard", 0, 0).reshape(shards * rows, piece)
    with jax.named_scope("window_core"):
        window, new_momentum, *blocks = lax.optimization_barrier((window, new_momentum, *blocks))
        other = lax.ppermute(window, "replica", [(i, i ^ 1) for i in range(replicas)])
    with jax.named_scope("product"):
        size = shards * rows
        work = 2 * XS * count * size * piece
        first, rest = call(
            first_kernel,
            [
                jax.ShapeDtypeStruct((XS * count, size), F32),
                jax.ShapeDtypeStruct((XS * count, piece), BF16),
            ],
            *blocks,
            window,
            flops=work,
        )
        shape = (XS, count, size)
        ordered = call(
            second_kernel,
            jax.ShapeDtypeStruct(shape, BF16),
            rest,
            other,
            first,
            flops=work,
        )
    with jax.named_scope("sum_x"):
        groups = [[y * XS + i for i in range(XS)] for y in range(YS)]
        parts = lax.all_to_all(ordered, "shard", 0, 0, axis_index_groups=groups)
        projected = call(finish_kernel, jax.ShapeDtypeStruct(shape[1:], BF16), parts)
    return projected, new_momentum


def solution(mesh):
    in_specs = (
        P(("shard", "replica"), None),
        P("shard", None),
        P("replica", "shard", None),
        P("replica", "shard", None),
        P("replica", "shard", None, None),
    )
    out_specs = (P(("shard", "replica"), None), P("replica", "shard", None))
    return jax.shard_map(local, mesh=mesh, in_specs=in_specs, out_specs=out_specs, check_vma=False)
```

```python
import numpy as np

import jax
import jax.numpy as jnp
from jax import lax
from jax.experimental import pallas as pl
from jax.experimental.pallas import tpu as pltpu
from jax.sharding import PartitionSpec as P

GROUP = 64
TOPK = 4
DECAY = 0.999
STEP = 0.01
PAIR = 2 * GROUP
XS = 4
YS = 8
MEMBERS = 2 * XS
VMEM_BYTES = 60 * 1024 * 1024
F32 = jnp.float32
BF16 = jnp.bfloat16
HIGH = lax.Precision.HIGHEST


def pair_table():
    k = np.arange(GROUP, dtype=np.float64)[:, None]
    n = np.arange(GROUP, dtype=np.float64)[None, :]
    c = np.cos(np.pi * (2.0 * n + 1.0) * k / (2.0 * GROUP)) * np.sqrt(2.0 / GROUP)
    c = c * np.where(k == 0, np.sqrt(0.5), 1.0)
    both = np.zeros((PAIR, PAIR), np.float64)
    both[:GROUP, :GROUP] = c
    both[GROUP:, GROUP:] = c
    return both.astype(np.float32)


def contract(a, b, da, db):
    return lax.dot_general(a, b, (((da,), (db,)), ((), ())), precision=HIGH, preferred_element_type=F32)


def forward_kernel(arrived, far):
    far[0] = arrived[2]


def own_kernel(tokens, own, sems):
    x = lax.axis_index("shard") % XS
    piece = own.shape[2]
    halves = [pl.multiple_of((h * XS + x) * piece, 128) for h in range(2)]
    for copy in fetch([(tokens.at[:, pl.ds(at, piece)], own.at[h]) for h, at in enumerate(halves)], sems):
        copy.wait()


def lay_out(indices, lanes):
    rows, _, groups = indices.shape
    spread = lax.broadcasted_iota(jnp.int32, (rows, lanes), 1) % rows
    spread = jnp.where(spread == lax.broadcasted_iota(jnp.int32, (rows, lanes), 0), 1.0, 0.0).astype(BF16)
    pair = lax.broadcasted_iota(jnp.int32, (groups, lanes), 1) // rows
    transform = lax.broadcasted_iota(jnp.int32, (groups, lanes), 0)
    spreads = [
        lax.dot_general(
            indices[:, j, :].astype(F32).astype(BF16), spread, (((0,), (0,)), ((), ())), preferred_element_type=F32
        )
        for j in range(TOPK)
    ]
    return [
        jnp.sum(jnp.where(transform == 2 * pair + side, spreads[j], 0.0), axis=0, keepdims=True)
        for side in range(2)
        for j in range(TOPK)
    ]


def choose(momentum, gradient, index, table):
    rows, width = momentum.shape
    pairs = width // PAIR
    lanes = pairs * rows
    blended = DECAY * momentum + gradient.astype(F32)
    stacked = jnp.concatenate([blended[:, p * PAIR : (p + 1) * PAIR] for p in range(pairs)], axis=0)
    spectra = contract(table, stacked, 1, 1)
    freq = lax.broadcasted_iota(jnp.int32, (GROUP, lanes), 0).astype(F32)
    picked = []
    for side in range(2):
        part = spectra[side * GROUP : (side + 1) * GROUP]
        picked += [jnp.where(freq == index[side * TOPK + j], part, 0.0) for j in range(TOPK)]
    return blended, picked


def fetch(pairs, sems):
    copies = [pltpu.make_async_copy(a, b, sems.at[i]) for i, (a, b) in enumerate(pairs)]
    for copy in copies:
        copy.start()
    return copies


def send_kernel(momentum, gradient, indices, table, send, mom, grad, ind, tab, sems):
    first, *loads = fetch([(indices, ind), (momentum, mom), (gradient, grad), (table, tab)], sems)
    first.wait()
    index = lay_out(ind, mom.shape[1] * mom.shape[2] // PAIR)
    for load in loads:
        load.wait()
    _, picked = choose(mom[0], grad[0], index, tab[...])
    values = [jnp.sum(p, axis=0, keepdims=True) for p in picked]
    message = jnp.concatenate(values + index, axis=0).astype(BF16)
    half = message.shape[1] // 2
    for r in range(send.shape[0]):
        send[r] = message[:, r % 2 * half : (r % 2 + 1) * half]


def cut_kernel(tokens, ahead, behind, cut, sems):
    x = lax.axis_index("shard") % XS
    piece = cut.shape[2]
    pieces = []
    for i, (d, h) in enumerate([(1, 0), (1, 1), (2, 0), (3, 0), (3, 1), (2, 1)]):
        at = pl.multiple_of((h * XS + (x + d) % XS) * piece, 128)
        pieces.append((tokens.at[:, pl.ds(at, piece)], cut.at[i]))
    cuts = fetch(pieces, sems)
    outs = []
    for i, (first, number, out) in enumerate([(0, 3, ahead), (3, 3, behind)]):
        for c in cuts[first : first + number]:
            c.wait()
        outs += fetch([(cut.at[pl.ds(first, number)], out)], sems.at[pl.ds(len(pieces) + i, 1)])
    for out in outs:
        out.wait()


def remain_kernel(momentum, gradient, indices, table, new_momentum, mom, grad, ind, tab, sems):
    for load in fetch([(momentum, mom), (gradient, grad), (indices, ind), (table, tab)], sems):
        load.wait()
    rows = mom.shape[1]
    index = lay_out(ind, rows * mom.shape[2] // PAIR)
    blended, picked = choose(mom[0], grad[0], index, tab[...])
    kept = [sum(picked[side * TOPK + 1 : (side + 1) * TOPK], picked[side * TOPK]) for side in range(2)]
    field = contract(jnp.concatenate(kept, axis=0), tab[...], 0, 0)
    for p in range(blended.shape[1] // PAIR):
        at = slice(p * PAIR, (p + 1) * PAIR)
        new_momentum[0, :, at] = blended[:, at] - field[p * rows : (p + 1) * rows]


def renew_kernel(received, weight, table, renewed):
    replicas, _, lanes = received.shape
    rows = weight.shape[0]
    half = weight.shape[1] // 2
    core = lax.axis_index("replica") % 2
    freq = lax.broadcasted_iota(jnp.int32, (GROUP, 128), 0).astype(F32).astype(BF16)
    columns = []
    for c in range(lanes // 128):
        at = slice(c * 128, (c + 1) * 128)
        sums = [jnp.zeros((GROUP, 128), F32) for _ in range(2)]
        for r in range(replicas):
            message = received[r, :, at]
            for side in range(2):
                dense = jnp.zeros((GROUP, 128), BF16)
                for row in range(side * TOPK, (side + 1) * TOPK):
                    dense = jnp.where(freq == message[2 * TOPK + row][None, :], message[row][None, :], dense)
                sums[side] = sums[side] + dense.astype(F32)
        columns.append(jnp.concatenate(sums, axis=0))
    field = contract(jnp.concatenate(columns, axis=1), table[...], 0, 0)
    old = weight[:, pl.ds(pl.multiple_of(core * half, 128), half)].astype(F32)
    per = half // XS // PAIR
    for x in range(XS):
        for p in range(per):
            q = x * per + p
            new = old[:, q * PAIR : (q + 1) * PAIR] - STEP * field[q * rows : (q + 1) * rows]
            new = new.astype(BF16)
            for y in range(YS):
                renewed[y * XS + x, :, p * PAIR : (p + 1) * PAIR] = new


def stack(own, ahead, far0, far1, behind, h):
    return jnp.concatenate([own[h], ahead[h], jnp.where(h == 0, far0[0], far1[0]), behind[h]], axis=0)


def product(tokens, window):
    return lax.dot_general(tokens, window[...], (((1,), (1,)), ((), ())), preferred_element_type=F32)


def first_kernel(*refs):
    *blocks, window, out, rest = refs
    core = lax.axis_index("replica") % 2
    out[...] = product(stack(*blocks, core), window)
    rest[...] = stack(*blocks, 1 - core)


def second_kernel(rest, window, first, out):
    x = lax.axis_index("shard") % XS
    count = out.shape[1]
    total = first[...] + product(rest[...], window)
    for d in range(XS):
        out[(x + XS - d) % XS] = total[d * count : (d + 1) * count].astype(BF16)


def finish_kernel(parts, out):
    total = parts[0].astype(F32)
    for x in range(1, XS):
        total = total + parts[x].astype(F32)
    out[...] = total.astype(BF16)


def call(kernel, out, *args, flops=0):
    out_list = jax.tree.leaves(out)
    moved = sum(a.size * a.dtype.itemsize for a in args) + sum(o.size * o.dtype.itemsize for o in out_list)
    return pl.pallas_call(
        kernel,
        out_shape=out,
        in_specs=[pl.BlockSpec(memory_space=pltpu.VMEM)] * len(args),
        out_specs=jax.tree.map(lambda _: pl.BlockSpec(memory_space=pltpu.VMEM), out),
        compiler_params=pltpu.CompilerParams(vmem_limit_bytes=20 * 1024 * 1024),
        cost_estimate=pl.CostEstimate(flops=flops, bytes_accessed=moved, transcendentals=0),
    )(*args)


def local(tokens, weight, momentum, gradient, indices):
    count, width = tokens.shape
    rows = weight.shape[0]
    half, piece = width // 2, width // 2 // XS
    table = jnp.asarray(pair_table())
    replicas = lax.axis_size("replica")
    shards = lax.axis_size("shard")

    lanes = width // PAIR * rows
    ordered_indices = indices[0].transpose(0, 2, 1)
    local_scratch = [
        pltpu.VMEM(momentum.shape, F32),
        pltpu.VMEM(gradient.shape, BF16),
        pltpu.VMEM(ordered_indices.shape, jnp.int32),
        pltpu.VMEM(table.shape, F32),
    ]
    hbm, vmem = pl.BlockSpec(memory_space=pltpu.HBM), pl.BlockSpec(memory_space=pltpu.VMEM)
    params = pltpu.CompilerParams(vmem_limit_bytes=VMEM_BYTES)
    with jax.named_scope("coefficients"):
        send = pl.pallas_call(
            send_kernel,
            out_shape=jax.ShapeDtypeStruct((replicas, 4 * TOPK, lanes // 2), BF16),
            in_specs=[hbm] * 4,
            out_specs=vmem,
            scratch_shapes=local_scratch + [pltpu.SemaphoreType.DMA((4,))],
            compiler_params=params,
            cost_estimate=pl.CostEstimate(flops=10**8, bytes_accessed=10**6, transcendentals=0),
        )(momentum, gradient, ordered_indices, table)
    with jax.named_scope("cut"):
        tokens, send = lax.optimization_barrier((tokens, send))
        ahead, behind = pl.pallas_call(
            cut_kernel,
            out_shape=[jax.ShapeDtypeStruct((n, count, piece), BF16) for n in (3, 3)],
            in_specs=[hbm],
            out_specs=[hbm] * 2,
            scratch_shapes=[pltpu.VMEM((6, count, piece), BF16), pltpu.SemaphoreType.DMA((8,))],
            compiler_params=params,
            cost_estimate=pl.CostEstimate(flops=0, bytes_accessed=4 * tokens.size, transcendentals=0),
        )(tokens)

    with jax.named_scope("exchange"):
        received = lax.all_to_all(send, "replica", 0, 0)
    with jax.named_scope("renew"):
        renewed = call(
            renew_kernel,
            jax.ShapeDtypeStruct((shards, rows, piece), BF16),
            received,
            weight,
            table,
            flops=10**10,
        )
    with jax.named_scope("tokens_x"):
        on, back = (
            [(s, s // XS * XS + (s + step) % XS) for s in range(shards)] for step in (1, XS - 1)
        )
        ahead = lax.ppermute(ahead, "shard", on)
        behind = lax.ppermute(behind, "shard", back)
        one = jax.ShapeDtypeStruct((1, count, piece), BF16)
        far0, far1 = (call(forward_kernel, one, arrived, flops=5 * 10**10) for arrived in (ahead, behind))
        momentum, _ = lax.optimization_barrier((momentum, far1))
        far0 = lax.ppermute(far0, "shard", on)
        far1 = lax.ppermute(far1, "shard", back)
        tokens, far0 = lax.optimization_barrier((tokens, far0))
        own = pl.pallas_call(
            own_kernel,
            out_shape=jax.ShapeDtypeStruct((2, count, piece), BF16),
            in_specs=[hbm],
            out_specs=vmem,
            scratch_shapes=[pltpu.SemaphoreType.DMA((2,))],
            compiler_params=pltpu.CompilerParams(vmem_limit_bytes=20 * 1024 * 1024),
            cost_estimate=pl.CostEstimate(flops=0, bytes_accessed=4 * count * piece, transcendentals=0),
        )(tokens)
        blocks = (own, ahead, far0, far1, behind)
    with jax.named_scope("momentum"):
        new_momentum = pl.pallas_call(
            remain_kernel,
            out_shape=jax.ShapeDtypeStruct(momentum.shape, F32),
            in_specs=[hbm] * 4,
            out_specs=vmem,
            scratch_shapes=local_scratch + [pltpu.SemaphoreType.DMA((4,))],
            compiler_params=pltpu.CompilerParams(vmem_limit_bytes=40 * 1024 * 1024),
            cost_estimate=pl.CostEstimate(flops=10**9, bytes_accessed=10**6, transcendentals=0),
        )(momentum, gradient, ordered_indices, table)
    with jax.named_scope("window"):
        window = lax.all_to_all(renewed, "shard", 0, 0).reshape(shards * rows, piece)
    with jax.named_scope("window_core"):
        window, new_momentum, *blocks = lax.optimization_barrier((window, new_momentum, *blocks))
        other = lax.ppermute(window, "replica", [(i, i ^ 1) for i in range(replicas)])
    with jax.named_scope("product"):
        size = shards * rows
        work = 2 * XS * count * size * piece
        first, rest = call(
            first_kernel,
            [
                jax.ShapeDtypeStruct((XS * count, size), F32),
                jax.ShapeDtypeStruct((XS * count, piece), BF16),
            ],
            *blocks,
            window,
            flops=work,
        )
        shape = (XS, count, size)
        ordered = call(
            second_kernel,
            jax.ShapeDtypeStruct(shape, BF16),
            rest,
            other,
            first,
            flops=work,
        )
    with jax.named_scope("sum_x"):
        groups = [[y * XS + i for i in range(XS)] for y in range(YS)]
        parts = lax.all_to_all(ordered, "shard", 0, 0, axis_index_groups=groups)
        projected = call(finish_kernel, jax.ShapeDtypeStruct(shape[1:], BF16), parts)
    return projected, new_momentum


def solution(mesh):
    in_specs = (
        P(("shard", "replica"), None),
        P("shard", None),
        P("replica", "shard", None),
        P("replica", "shard", None),
        P("replica", "shard", None, None),
    )
    out_specs = (P(("shard", "replica"), None), P("replica", "shard", None))
    return jax.shard_map(local, mesh=mesh, in_specs=in_specs, out_specs=out_specs, check_vma=False)
```
